256 devices in a mesh: tile: 64 (over x, z, core), chan: 4 (over y).
Axes of the slice: x: 4, y: 4, z: 8, core: 2. Of those that a mesh axis runs over, the one named last changes fastest.
Arguments:
- visibility: bfloat16 [1024, 2, 8, 512], P('tile', None, 'chan'), may hold values from -6 to 6
- imaging_weight: bfloat16 [1024, 8, 512], P('tile', 'chan'), may hold values from 0.19921875 to 5
- position: int32 [1024, 2, 512], P('tile'), may hold values from 0 to 3615
- anchor: int32 [1024, 2], P('tile'), may hold values from 0 to 128
- destination: int32 [1024], P('tile'), may hold values from 0 to 63, as said below
- block_count: int32 [64], P('tile'), may hold values from 12 to 16, as said below
- kernel: float32 [32, 16], replicated, may hold values from 0.25 to 1.5
Outputs:
- combined_grid: float32 [2, 16384, 256], P(None, ('tile', 'chan'))
- residual: bfloat16 [1024, 2, 8, 512], P('tile', None, 'chan')
The draws below stay inside these ranges and needn't reach their ends.
Inputs may be any that keep to these rules, and one draw needn't show every extreme that they name: `destination`: among each owner's 16 blocks at most 2 name one tile; one tile is named by exactly 2 blocks of every owner, all of them among that owner's first 8 blocks. Owner i's live blocks are its first block_count[i]; some owner has all 16 live. `position`: every entry is below 2^12. A program may carry positions, corners and other integer fields packed into fewer bits when they are sent, as long as nothing is lost.
All inputs are finite; a program needn't handle non-finite values.
Results may differ from the reference program's by a relative error of at most 0.009.
Values may be sent and summed in bfloat16 or wider, within the bound.
A program may use at most 64 MiB of HBM per device.

```python
import math
import jax
import jax.numpy as jnp
import numpy as np
from jax import lax

BLOCK = 512
TAPS = 16
OS = 32
SUB = 128
TS = 256
BLK_DEV = 16
CAP = 2
BLOCKS = 1024
CH = 8
N_TILE = 64


def draw_destination(key, part):
    base = jax.random.fold_in(key, 17)
    busy_key, favor_key, device_key = jax.random.split(base, 3)
    busiest = jax.random.randint(busy_key, (), 0, N_TILE)
    favored = (jax.random.randint(favor_key, (N_TILE,), 0, 4) == 0).astype(jnp.int32)
    pool_size = (N_TILE - 1) * CAP
    slot_ids = jnp.arange(pool_size, dtype=jnp.int32)
    pool_tile = slot_ids // CAP
    pool_tile = jnp.where(pool_tile >= busiest, pool_tile + 1, pool_tile)

    def one_device(dev_key):
        score_key, front_key, back_key = jax.random.split(dev_key, 3)
        levels = jax.random.randint(score_key, (pool_size,), 0, 1 << 16)
        scores = levels // (1 + 3 * favored[pool_tile]) * pool_size + slot_ids
        picked = pool_tile[jnp.argsort(scores)[:BLK_DEV - CAP]]
        rows_all = jnp.concatenate([jnp.full((CAP,), busiest, jnp.int32), picked.astype(jnp.int32)])
        front = jax.random.permutation(front_key, BLK_DEV // 2)
        behind = jax.random.permutation(back_key, BLK_DEV - BLK_DEV // 2) + BLK_DEV // 2
        placing = jnp.concatenate([front, behind])
        return rows_all[placing]
    every = jax.vmap(one_device)(jax.random.split(device_key, N_TILE))
    return every.reshape(N_TILE * BLK_DEV).astype(jnp.int32)


def draw_block_count(key, part):
    first_key, second_key = jax.random.split(jax.random.fold_in(key, 5))
    counts = jax.random.randint(first_key, (N_TILE,), BLK_DEV * 3 // 4, BLK_DEV + 1)
    fullest = jax.random.randint(second_key, (), 0, N_TILE)
    return jnp.where(jnp.arange(N_TILE) == fullest, BLK_DEV, counts).astype(jnp.int32)


def touch_ends(array, stream_key, smallest, high):
    spot = [jax.random.randint(jax.random.fold_in(stream_key, axis), (), 0, length) for axis, length in enumerate(array.shape)]
    longest = array.shape.index(max(array.shape))
    beside = spot[:longest] + [(spot[longest] + 1) % array.shape[longest]] + spot[longest + 1:]
    return array.at[tuple(spot)].set(smallest).at[tuple(beside)].set(high)


def block_levels(stream_key, shape, cuts, smallest, largest):
    gain, own = 1.0, jax.random.fold_in(stream_key, 6)
    for dim, parts in cuts:
        steps = jnp.exp(jax.random.uniform(jax.random.fold_in(own, dim), (parts,), jnp.float32, smallest / len(cuts), largest / len(cuts)))
        gain = gain * jnp.repeat(steps, shape[dim] // parts).reshape([-1 if axis == dim else 1 for axis in range(len(shape))])
    return gain


def normal_values(stream_key, shape, deviation, bound, cuts=(), kind=jnp.bfloat16):
    gain = block_levels(stream_key, shape, cuts, -0.22, 0.18) if cuts else 1.0
    array = jax.random.normal(stream_key, shape, jnp.float32) * deviation * gain
    return jnp.minimum(jnp.maximum(array, -bound), bound).astype(kind)


def setup_inputs(seed: int = 0) -> dict:
    streams_of = jax.random.split(jax.random.key(seed), 8)
    visibility = normal_values(streams_of[0], (BLOCKS, 2, CH, BLOCK), 1.0, 6.0, ((0, 64), (2, 4)))
    imaging_weight = jnp.clip(jnp.exp(math.log(5.0) - 3.2227897 * jax.random.uniform(streams_of[1], (BLOCKS, CH, BLOCK), jnp.float32) ** block_levels(streams_of[1], (BLOCKS, CH, BLOCK), ((0, 64), (1, 4)), -0.2, 0.2)), 0.19921875, 5.0).astype(jnp.bfloat16)
    position = touch_ends(jax.random.randint(streams_of[2], (BLOCKS, 2, BLOCK), 0, (SUB - TAPS + 1) * OS), jax.random.fold_in(streams_of[2], 1), 0, ((SUB - TAPS + 1) * OS) - 1).astype(jnp.int32)
    anchor = touch_ends(jax.random.randint(streams_of[3], (BLOCKS, 2), 0, TS - SUB + 1), jax.random.fold_in(streams_of[3], 1), 0, TS - SUB).astype(jnp.int32)
    destination = draw_destination(jax.random.fold_in(streams_of[7], 71), 0)
    block_count = draw_block_count(jax.random.fold_in(streams_of[7], 71), 0)
    kernel = jnp.clip(jax.random.uniform(streams_of[6], (OS, TAPS), jnp.float32, 0.25, 1.5), 0.25, 1.5)
    return {"visibility": visibility, "imaging_weight": imaging_weight, "position": position, "anchor": anchor, "destination": destination, "block_count": block_count, "kernel": kernel}


def tap_matrix(positions, kernel):
    cell_row = positions // OS
    offset = positions % OS
    tap_values = kernel[offset]
    cell_ids = jnp.arange(SUB, dtype=jnp.int32)
    distance = cell_ids[:, None] - cell_row[None, :]
    matrix = jnp.zeros((SUB, positions.shape[0]), jnp.float32)
    for tap_index in range(TAPS):
        matrix = matrix + jnp.where(distance == tap_index, tap_values[:, tap_index][None, :], jnp.float32(0.0))
    return matrix.astype(jnp.bfloat16)


def reference(visibility, imaging_weight, position, anchor, destination, block_count, kernel):
    channels = visibility.shape[2]
    block_ids = jnp.arange(visibility.shape[0], dtype=jnp.int32)
    is_live = (block_ids % BLK_DEV) < block_count[block_ids // BLK_DEV]
    anchor_zero = jnp.zeros((), jnp.int32)

    def grid_one(tile_grid, block_item):
        values, weights, positions, corner, target, alive = block_item
        row_taps = tap_matrix(positions[0], kernel)
        col_taps = tap_matrix(positions[1], kernel)
        scaled = values.astype(jnp.float32) * weights.astype(jnp.float32)[None]
        weighted = (scaled[..., None] * col_taps.T.astype(jnp.float32)[None, None]).astype(jnp.bfloat16)
        patches = jnp.einsum('iv,rcvj->rcij', row_taps.astype(jnp.float32), weighted.astype(jnp.float32))
        patches = jnp.where(alive, patches, jnp.float32(0.0))
        start_at = (target.astype(jnp.int32), anchor_zero, anchor_zero, corner[0].astype(jnp.int32), corner[1].astype(jnp.int32))
        current = lax.dynamic_slice(tile_grid, start_at, (1, 2, channels, SUB, SUB))
        tile_grid = lax.dynamic_update_slice(tile_grid, current + patches[None], start_at)
        return tile_grid, None

    tile_grid = jnp.zeros((N_TILE, 2, channels, TS, TS), jnp.float32)
    tile_grid, _ = lax.scan(grid_one, tile_grid, (visibility, imaging_weight, position, anchor, destination, is_live))
    partner_ids = np.arange(N_TILE) ^ (N_TILE // 2)
    flipped = tile_grid[partner_ids][..., ::-1, ::-1]
    symmetric = jnp.concatenate([tile_grid[:, 0:1] + flipped[:, 0:1], tile_grid[:, 1:2] - flipped[:, 1:2]], axis=1)
    combined_grid = jnp.sum(symmetric, axis=2).transpose(1, 0, 2, 3).reshape(2, N_TILE * TS, TS)

    def degrid_one(block_item):
        positions, corner, target, alive = block_item
        row_taps = tap_matrix(positions[0], kernel)
        col_taps = tap_matrix(positions[1], kernel)
        start_at = (target.astype(jnp.int32), anchor_zero, anchor_zero, corner[0].astype(jnp.int32), corner[1].astype(jnp.int32))
        window = lax.dynamic_slice(symmetric, start_at, (1, 2, channels, SUB, SUB))[0].astype(jnp.bfloat16)
        product = jnp.einsum('iv,rcij->rcvj', row_taps.astype(jnp.float32), window.astype(jnp.float32))
        predicted = jnp.sum(product * col_taps.T.astype(jnp.float32)[None, None], axis=-1) / (TAPS * TAPS)
        return jnp.where(alive, predicted, jnp.float32(0.0)).astype(jnp.bfloat16)

    predicted = lax.map(degrid_one, (position, anchor, destination, is_live))
    residual = (visibility.astype(jnp.float32) - predicted.astype(jnp.float32)).astype(jnp.bfloat16)
    return combined_grid, residual
```

```python
import functools

import jax
import jax.numpy as jnp
from jax import lax
from jax.experimental import pallas as pl
from jax.experimental.pallas import tpu as pltpu
from jax.sharding import PartitionSpec as P

TAPS = 16
OS = 32
SUB = 128
TS = 256
TILES = 64
CHAN = 4
SLOTS = 128
ROWS = 144
GROUPS = 4
LIMIT = 40 * 1024 * 1024

VMEM = pl.BlockSpec(memory_space=pltpu.VMEM)
SMEM = pl.BlockSpec(memory_space=pltpu.SMEM)
MESH = pl.DeviceIdType.MESH


def sort_kernel(dest, count, anchor, vis, weight, pos, scaled, packed, info, used):
    me = lax.axis_index("tile")
    turn = me + (me >> 2) + (me >> 4)
    scaled[...] = jnp.zeros(scaled.shape, scaled.dtype)
    packed[...] = jnp.zeros(packed.shape, packed.dtype)
    for quad in range(TILES // 4):
        used[quad] = 0
    half = lax.broadcasted_iota(jnp.int32, (8, 128), 0) // GROUPS
    for b in range(16):
        alive = (b < count[0]).astype(jnp.int32)
        tile = dest[b]
        quad = (tile & 31) >> 1
        rank = used[quad]
        used[quad] = rank + alive
        member = (rank + turn) & 3
        device = (quad << 1) | (member & 1) | ((member >> 1) << 5)
        which = rank >> 2
        mirror = tile >> 5
        flip = 1 - 2 * mirror
        top = mirror * (TS - SUB) + flip * anchor[2 * b]
        left = mirror * (TS - SUB) + flip * anchor[2 * b + 1]
        base = jnp.minimum(top >> 4, 7)
        info[b] = (device * 2 + which) | (mirror << 8) | (alive << 9)
        meta = (alive << 26) | (base << 27) | (mirror << 30) | ((tile & 1) << 31)

        @pl.when(alive == 1)
        def _():
            place = pos[b]
            cell = mirror * (SUB - TAPS) + flip * (place >> 5)
            offset = place & (OS - 1)
            row = (cell[:4] + (top - base * 16)) * OS + offset[:4]
            column = (cell[4:] + left) * OS + offset[4:]
            word = row | (column << 13) | meta
            both = jnp.concatenate([word, word], axis=0)
            packed[device] = jnp.where(half == which, both, packed[device])
            values = vis[b].astype(jnp.float32)
            factor = weight[b].astype(jnp.float32)
            sign = flip.astype(jnp.float32)
            scaled[device * 2 + which] = jnp.concatenate(
                [values[:8] * factor, values[8:] * factor * sign], axis=0
            ).astype(jnp.bfloat16)


def sort_blocks(dest, count, anchor, vis, weight, pos):
    return pl.pallas_call(
        sort_kernel,
        out_shape=(
            jax.ShapeDtypeStruct((SLOTS, 16, 128), jnp.bfloat16),
            jax.ShapeDtypeStruct((TILES, 8, 128), jnp.int32),
            jax.ShapeDtypeStruct((16,), jnp.int32),
        ),
        in_specs=[SMEM, SMEM, SMEM, VMEM, VMEM, VMEM],
        out_specs=(VMEM, VMEM, SMEM),
        scratch_shapes=[pltpu.SMEM((TILES // 4,), jnp.int32)],
        name="sort_blocks",
    )(dest, count, anchor, vis, weight, pos)


def greet_tiles(me):
    barrier = pltpu.get_barrier_semaphore()

    def greet(step, carry):
        pl.semaphore_signal(
            barrier, inc=1, device_id={"tile": (me + step) % TILES}, device_id_type=MESH
        )
        return carry

    lax.fori_loop(1, TILES, greet, 0)
    return barrier


def route_kernel(scaled, packed, got_scaled, got_packed, s_out, s_in, p_out, p_in, here):
    me = lax.axis_index("tile")
    pl.semaphore_wait(greet_tiles(me), TILES - 1)

    def copies(peer):
        first = pltpu.make_async_remote_copy(
            src_ref=scaled.at[pl.ds(peer * 2, 2)],
            dst_ref=got_scaled.at[pl.ds(me * 2, 2)],
            send_sem=s_out.at[peer],
            recv_sem=s_in.at[me],
            device_id={"tile": peer},
            device_id_type=MESH,
        )
        second = pltpu.make_async_remote_copy(
            src_ref=packed.at[pl.ds(peer, 1)],
            dst_ref=got_packed.at[pl.ds(me, 1)],
            send_sem=p_out.at[peer],
            recv_sem=p_in.at[me],
            device_id={"tile": peer},
            device_id_type=MESH,
        )
        return first, second

    def send(step, carry):
        first, second = copies((me + step) % TILES)
        first.start()
        second.start()
        return carry

    lax.fori_loop(1, TILES, send, 0)
    own_scaled = pltpu.make_async_copy(
        scaled.at[pl.ds(me * 2, 2)], got_scaled.at[pl.ds(me * 2, 2)], here.at[0]
    )
    own_packed = pltpu.make_async_copy(
        packed.at[pl.ds(me, 1)], got_packed.at[pl.ds(me, 1)], here.at[1]
    )
    own_scaled.start()
    own_packed.start()
    own_scaled.wait()
    own_packed.wait()

    def finish(step, carry):
        peer = (me + step) % TILES
        pltpu.make_async_copy(
            got_scaled.at[pl.ds(peer * 2, 2)], got_scaled.at[pl.ds(peer * 2, 2)], s_in.at[peer]
        ).wait()
        pltpu.make_async_copy(
            got_packed.at[pl.ds(peer, 1)], got_packed.at[pl.ds(peer, 1)], p_in.at[peer]
        ).wait()
        first, second = copies(peer)
        first.wait_send()
        second.wait_send()
        return carry

    lax.fori_loop(1, TILES, finish, 0)


def route(scaled, packed):
    return pl.pallas_call(
        route_kernel,
        out_shape=(
            jax.ShapeDtypeStruct(scaled.shape, scaled.dtype),
            jax.ShapeDtypeStruct(packed.shape, packed.dtype),
        ),
        in_specs=[VMEM, VMEM],
        out_specs=(VMEM, VMEM),
        scratch_shapes=[pltpu.SemaphoreType.DMA((TILES,))] * 4 + [pltpu.SemaphoreType.DMA((2,))],
        compiler_params=pltpu.CompilerParams(
            collective_id=0, has_side_effects=True, vmem_limit_bytes=LIMIT
        ),
        name="route",
    )(scaled, packed)


def gather_live(meta, order):
    def look(slot, count):
        order[count] = slot
        return count + ((meta[slot] >> 26) & 1)

    count = lax.fori_loop(0, SLOTS, look, jnp.int32(0))
    return count


def tap_rows(table, cell, column, pieces):
    cell = jnp.broadcast_to(cell, (8, 128))
    column = jnp.broadcast_to(column, (8, 128))
    low = jnp.take_along_axis(table[:8], column, axis=1, mode="promise_in_bounds")
    high = jnp.take_along_axis(table[8:], column, axis=1, mode="promise_in_bounds")
    sub = lax.broadcasted_iota(jnp.int32, (8, 128), 0)
    part = cell & 7
    whole = cell >> 3
    turn = (sub - part) & 7
    low = jnp.take_along_axis(low, turn, axis=0, mode="promise_in_bounds")
    high = jnp.take_along_axis(high, turn, axis=0, mode="promise_in_bounds")
    after = sub >= part
    zero = jnp.zeros((8, 128), jnp.float32)
    first = jnp.where(after, low, zero)
    second = jnp.where(after, high, low)
    third = jnp.where(after, zero, high)
    at = [whole == m for m in range(pieces)]
    rows = []
    for m in range(pieces):
        value = zero
        if m >= 2:
            value = jnp.where(at[m - 2], third, value)
        if m >= 1:
            value = jnp.where(at[m - 1], second, value)
        rows.append(jnp.where(at[m], first, value))
    return jnp.concatenate(rows, axis=0)


def slot_taps(packed, table, slot, word):
    both = packed[slot >> 1]
    mine = jnp.where((slot & 1) == 1, both[4:], both[:4])
    shift = OS * ((word >> 30) & 1)
    row_cell = (mine >> 5) & 255
    row_column = (mine & (OS - 1)) + shift
    col_cell = (mine >> 18) & 255
    col_column = ((mine >> 13) & (OS - 1)) + shift
    rows = [
        tap_rows(table, row_cell[g : g + 1], row_column[g : g + 1], ROWS // 8)
        for g in range(GROUPS)
    ]
    cols = [
        tap_rows(table, col_cell[g : g + 1], col_column[g : g + 1], TS // 8).astype(jnp.bfloat16)
        for g in range(GROUPS)
    ]
    return rows, jnp.concatenate(cols, axis=1)


def grid_kernel(meta, scaled, packed, table, grid, order):
    count = gather_live(meta, order)
    grid[...] = jnp.zeros(grid.shape, grid.dtype)
    taps = table[...]

    def one(slot, keep):
        word = meta[slot]
        rows, cols = slot_taps(packed, taps, slot, word)
        values = scaled[slot].astype(jnp.float32) * keep
        planes = []
        for plane in range(4):
            parts = [
                (rows[g] * values[plane * GROUPS + g : plane * GROUPS + g + 1]).astype(jnp.bfloat16)
                for g in range(GROUPS)
            ]
            planes.append(jnp.concatenate(parts, axis=1))
        left = jnp.concatenate(planes, axis=0)
        product = lax.dot_general(
            left, cols, (((1,), (1,)), ((), ())), preferred_element_type=jnp.float32
        )
        which = (word >> 31) & 1
        start = pl.multiple_of(((word >> 27) & 7) * 16, 16)
        for plane in range(4):
            grid[which, plane, pl.ds(start, ROWS), :] += product[plane * ROWS : (plane + 1) * ROWS]

    def step(turn, carry):
        one(order[2 * turn], jnp.float32(1.0))
        later = 2 * turn + 1
        extra = later < count
        one(order[jnp.where(extra, later, 0)], extra.astype(jnp.float32))
        return carry

    lax.fori_loop(0, (count + 1) >> 1, step, 0)


def grid_blocks(meta, scaled, packed, table):
    return pl.pallas_call(
        grid_kernel,
        out_shape=jax.ShapeDtypeStruct((2, 4, TS, TS), jnp.float32),
        in_specs=[SMEM, VMEM, VMEM, VMEM],
        out_specs=VMEM,
        scratch_shapes=[pltpu.SMEM((SLOTS + 8,), jnp.int32)],
        compiler_params=pltpu.CompilerParams(vmem_limit_bytes=LIMIT),
        name="grid_blocks",
    )(meta, scaled, packed, table)


def join_kernel(grid, whole, summed, half, got_half, total, mine, got_mine, send, recv):
    me = lax.axis_index("tile")
    core = me & 1
    near = me ^ 1
    far = me ^ (TILES // 2)
    barrier = pltpu.get_barrier_semaphore()
    for peer in (near, far):
        pl.semaphore_signal(barrier, inc=1, device_id={"tile": peer}, device_id_type=MESH)

    def pass_on(source, target, sem, peer):
        return pltpu.make_async_remote_copy(
            src_ref=source,
            dst_ref=target,
            send_sem=send.at[sem],
            recv_sem=recv.at[sem],
            device_id={"tile": peer},
            device_id_type=MESH,
        )

    pl.semaphore_wait(barrier, 2)
    first = [pass_on(half.at[k], got_half.at[k], k, near) for k in range(4)]
    second = [pass_on(mine.at[k], got_mine.at[k], 4 + k, far) for k in range(4)]
    third = [pass_on(whole.at[core, k], whole.at[core, k], 8 + k, near) for k in range(4)]
    for k in range(4):
        half[k] = grid[1 - core, k].astype(jnp.bfloat16)
        first[k].start()
    for k in range(4):
        first[k].wait_recv()
        value = grid[core, k] + got_half[k].astype(jnp.float32)
        total[k] = value
        mine[k] = value.astype(jnp.bfloat16)
        second[k].start()
    for k in range(4):
        second[k].wait_recv()
        value = total[k] + got_mine[k].astype(jnp.float32)
        whole[core, k] = value.astype(jnp.bfloat16)
        third[k].start()
        if k % 2 == 0:
            summed[k // 2] = value
        else:
            summed[k // 2] += value
    for k in range(4):
        other = pltpu.make_async_copy(whole.at[1 - core, k], whole.at[1 - core, k], recv.at[8 + k])
        other.wait()
        first[k].wait_send()
        second[k].wait_send()
        third[k].wait_send()


def join_grids(grid):
    return pl.pallas_call(
        join_kernel,
        out_shape=(
            jax.ShapeDtypeStruct((2, 4, TS, TS), jnp.bfloat16),
            jax.ShapeDtypeStruct((2, TS, TS), jnp.float32),
        ),
        in_specs=[VMEM],
        out_specs=(VMEM, VMEM),
        scratch_shapes=[
            pltpu.VMEM((4, TS, TS), jnp.bfloat16),
            pltpu.VMEM((4, TS, TS), jnp.bfloat16),
            pltpu.VMEM((4, TS, TS), jnp.float32),
            pltpu.VMEM((4, TS, TS), jnp.bfloat16),
            pltpu.VMEM((4, TS, TS), jnp.bfloat16),
            pltpu.SemaphoreType.DMA((12,)),
            pltpu.SemaphoreType.DMA((12,)),
        ],
        compiler_params=pltpu.CompilerParams(
            collective_id=1, has_side_effects=True, vmem_limit_bytes=LIMIT
        ),
        name="join_grids",
    )(grid)


def degrid_kernel(meta, packed, table, whole, predicted, order):
    count = gather_live(meta, order)
    taps = table[...]

    def one(slot):
        word = meta[slot]
        rows, cols = slot_taps(packed, taps, slot, word)
        which = (word >> 31) & 1
        start = pl.multiple_of(((word >> 27) & 7) * 16, 16)
        results = []
        for plane in range(4):
            window = whole[which, plane, pl.ds(start, ROWS), :]
            across = jnp.dot(window, cols, preferred_element_type=jnp.float32)
            for g in range(GROUPS):
                results.append(
                    jnp.sum(rows[g] * across[:, g * 128 : (g + 1) * 128], axis=0, keepdims=True)
                )
        scale = jnp.float32(1.0 / (TAPS * TAPS))
        predicted[slot] = (jnp.concatenate(results, axis=0) * scale).astype(jnp.bfloat16)

    def step(turn, carry):
        one(order[2 * turn])
        later = 2 * turn + 1
        one(order[jnp.where(later < count, later, 0)])
        return carry

    lax.fori_loop(0, (count + 1) >> 1, step, 0)


def degrid_blocks(meta, packed, table, whole):
    return pl.pallas_call(
        degrid_kernel,
        out_shape=jax.ShapeDtypeStruct((SLOTS, 16, 128), jnp.bfloat16),
        in_specs=[SMEM, VMEM, VMEM, VMEM],
        out_specs=VMEM,
        scratch_shapes=[pltpu.SMEM((SLOTS + 8,), jnp.int32)],
        compiler_params=pltpu.CompilerParams(vmem_limit_bytes=LIMIT),
        name="degrid_blocks",
    )(meta, packed, table, whole)


def back_kernel(
    info, predicted, vis, summed, residual, combined, back, parts, b_out, b_in, c_out, c_in, here
):
    me = lax.axis_index("tile")
    chan = lax.axis_index("chan")
    upper = me // (TILES // 2)
    barrier = greet_tiles(me)
    for k in range(1, CHAN):
        pl.semaphore_signal(
            barrier, inc=1, device_id={"chan": (chan + k) % CHAN}, device_id_type=MESH
        )
    pl.semaphore_wait(barrier, TILES - 1 + CHAN - 1)

    def rows_of(group):
        place = group + upper * (CHAN - 1 - 2 * group)
        return pl.ds(pl.multiple_of(place * (TS // CHAN), TS // CHAN), TS // CHAN)

    def across(k):
        group = (chan + k) % CHAN
        return pltpu.make_async_remote_copy(
            src_ref=summed.at[:, rows_of(group), :],
            dst_ref=parts.at[k - 1],
            send_sem=c_out.at[k - 1],
            recv_sem=c_in.at[k - 1],
            device_id={"chan": group},
            device_id_type=MESH,
        )

    def home(peer):
        return pltpu.make_async_remote_copy(
            src_ref=predicted.at[pl.ds(peer * 2, 2)],
            dst_ref=back.at[pl.ds(me * 2, 2)],
            send_sem=b_out.at[peer],
            recv_sem=b_in.at[me],
            device_id={"tile": peer},
            device_id_type=MESH,
        )

    def send(step, carry):
        home((me + step) % TILES).start()
        return carry

    for k in range(1, CHAN):
        across(k).start()
    lax.fori_loop(1, TILES, send, 0)
    own = pltpu.make_async_copy(
        predicted.at[pl.ds(me * 2, 2)], back.at[pl.ds(me * 2, 2)], here.at[0]
    )
    own.start()
    total = summed[:, rows_of(chan), :]
    for k in range(1, CHAN):
        across(k).wait()
        total = total + parts[k - 1]
    combined[...] = total
    own.wait()

    def finish(step, carry):
        peer = (me + step) % TILES
        pltpu.make_async_copy(
            back.at[pl.ds(peer * 2, 2)], back.at[pl.ds(peer * 2, 2)], b_in.at[peer]
        ).wait()
        home(peer).wait_send()
        return carry

    lax.fori_loop(1, TILES, finish, 0)
    lower = lax.broadcasted_iota(jnp.int32, (16, 128), 0) < 8
    for b in range(16):
        word = info[b]
        alive = ((word >> 9) & 1) == 1
        flip = (1 - 2 * ((word >> 8) & 1)).astype(jnp.float32)
        value = back[word & 127].astype(jnp.float32)
        value = jnp.where(lower, value, value * flip)
        value = jnp.where(alive, value, jnp.float32(0.0))
        residual[b] = (vis[b].astype(jnp.float32) - value).astype(jnp.bfloat16)


def send_back(info, predicted, vis, summed):
    return pl.pallas_call(
        back_kernel,
        out_shape=(
            jax.ShapeDtypeStruct((16, 16, 128), jnp.bfloat16),
            jax.ShapeDtypeStruct((2, TS // CHAN, TS), jnp.float32),
        ),
        in_specs=[SMEM, VMEM, VMEM, VMEM],
        out_specs=(VMEM, VMEM),
        scratch_shapes=[
            pltpu.VMEM((SLOTS, 16, 128), jnp.bfloat16),
            pltpu.VMEM((CHAN - 1, 2, TS // CHAN, TS), jnp.float32),
            pltpu.SemaphoreType.DMA((TILES,)),
            pltpu.SemaphoreType.DMA((TILES,)),
            pltpu.SemaphoreType.DMA((CHAN - 1,)),
            pltpu.SemaphoreType.DMA((CHAN - 1,)),
            pltpu.SemaphoreType.DMA((1,)),
        ],
        compiler_params=pltpu.CompilerParams(
            collective_id=2, has_side_effects=True, vmem_limit_bytes=LIMIT
        ),
        name="send_back",
    )(info, predicted, vis, summed)


def per_device(visibility, imaging_weight, position, anchor, destination, block_count, kernel):
    vis = visibility.reshape(16, 16, 128)
    weight = imaging_weight.reshape(16, 8, 128)
    pos = position.reshape(16, 8, 128)
    rounded = lax.reduce_precision(kernel, 8, 7).T
    table = jnp.concatenate([rounded, rounded[::-1], jnp.zeros((TAPS, 64), jnp.float32)], axis=1)
    scaled, packed, info = sort_blocks(
        destination, block_count, anchor.reshape(32), vis, weight, pos
    )
    scaled, packed = route(scaled, packed)
    meta = packed.reshape(TILES, 2, 4, 128)[:, :, 0, 0].reshape(SLOTS)
    grid = grid_blocks(meta, scaled, packed, table)
    whole, summed = join_grids(grid)
    predicted = degrid_blocks(meta, packed, table, whole)
    residual, combined = send_back(info, predicted, vis, summed)
    upper = lax.axis_index("tile") >= TILES // 2
    sign = jnp.array([1.0, -1.0], jnp.float32).reshape(2, 1, 1)
    combined = jnp.where(upper, combined[:, ::-1, ::-1] * sign, combined)
    return combined, residual.reshape(visibility.shape)


def solution(mesh):
    placed = (
        P("tile", None, "chan", None),
        P("tile", "chan", None),
        P("tile", None, None),
        P("tile", None),
        P("tile"),
        P("tile"),
        P(),
    )
    return jax.shard_map(
        per_device,
        mesh=mesh,
        in_specs=placed,
        out_specs=(P(None, ("tile", "chan"), None), P("tile", None, "chan", None)),
        check_vma=False,
    )
```

```python
import functools

import jax
import jax.numpy as jnp
from jax import lax
from jax.experimental import pallas as pl
from jax.experimental.pallas import tpu as pltpu
from jax.sharding import PartitionSpec as P

BLOCK = 512
TAPS = 16
OS = 32
SUB = 128
TS = 256
TILES = 64
CHAN = 4
SLOTS = 128
ROWS = 144
GROUPS = 4
LIMIT = 40 * 1024 * 1024

VMEM = pl.BlockSpec(memory_space=pltpu.VMEM)
SMEM = pl.BlockSpec(memory_space=pltpu.SMEM)
HBM = pl.BlockSpec(memory_space=pltpu.HBM)
MESH = pl.DeviceIdType.MESH


def sort_kernel(
    dest,
    count,
    anchor,
    far_vis,
    far_weight,
    far_pos,
    kernel,
    scaled,
    packed,
    info,
    table,
    used,
    vis,
    weight,
    pos,
    sems,
):
    fetches = [
        pltpu.make_async_copy(source, target, sems.at[k])
        for k, (source, target) in enumerate(((far_vis, vis), (far_weight, weight), (far_pos, pos)))
    ]
    for fetch in fetches:
        fetch.start()
    me = lax.axis_index("tile")
    turn = me + (me >> 2) + (me >> 4)
    scaled[...] = jnp.zeros(scaled.shape, scaled.dtype)
    packed[...] = jnp.zeros(packed.shape, packed.dtype)
    for quad in range(TILES // 4):
        used[quad] = 0

    def ones_where(mask):
        return jnp.where(mask, jnp.float32(1.0), jnp.float32(0.0)).astype(jnp.bfloat16)

    def iota(shape, axis):
        return lax.broadcasted_iota(jnp.int32, shape, axis)

    values = kernel[...].astype(jnp.bfloat16)
    swap = ones_where(iota((TAPS, TAPS), 0) + iota((TAPS, TAPS), 1) == TAPS - 1)
    turned = jnp.dot(swap, values, preferred_element_type=jnp.float32).astype(jnp.bfloat16)
    spread = iota((OS, 128), 1) - iota((OS, 128), 0)
    table[...] = jnp.dot(
        values, ones_where(spread == 0), preferred_element_type=jnp.float32
    ) + jnp.dot(turned, ones_where(spread == OS), preferred_element_type=jnp.float32)
    for fetch in fetches:
        fetch.wait()
    for b in range(16):
        alive = (b < count[0]).astype(jnp.int32)
        tile = dest[b]
        quad = (tile & 31) >> 1
        rank = used[quad]
        used[quad] = rank + alive
        member = (rank + turn) & 3
        device = (quad << 1) | (member & 1) | ((member >> 1) << 5)
        which = rank >> 2
        mirror = tile >> 5
        flip = 1 - 2 * mirror
        top = mirror * (TS - SUB) + flip * anchor[0, b]
        left = mirror * (TS - SUB) + flip * anchor[1, b]
        base = jnp.minimum(top >> 4, 7)
        info[b] = (device * 2 + which) | (mirror << 8) | (alive << 9)
        meta = (alive << 26) | (base << 27) | (mirror << 30) | ((tile & 1) << 31)

        @pl.when(alive == 1)
        def _():
            place = pos[b]
            cell = mirror * (SUB - TAPS) + flip * (place >> 5)
            offset = place & (OS - 1)
            row = (cell[0:1] + (top - base * 16)) * OS + offset[0:1]
            column = (cell[1:2] + left) * OS + offset[1:2]
            packed[device, pl.ds(which, 1), :] = row | (column << 13) | meta
            factor = weight[b].astype(jnp.float32)
            sign = flip.astype(jnp.float32)
            slot = device * 2 + which
            scaled[slot, 0] = (vis[b, 0].astype(jnp.float32) * factor).astype(jnp.bfloat16)
            scaled[slot, 1] = (vis[b, 1].astype(jnp.float32) * (factor * sign)).astype(jnp.bfloat16)


def sort_blocks(dest, count, anchor, vis, weight, pos, kernel):
    return pl.pallas_call(
        sort_kernel,
        out_shape=(
            jax.ShapeDtypeStruct((SLOTS, 2, 2, BLOCK), jnp.bfloat16),
            jax.ShapeDtypeStruct((TILES, 2, BLOCK), jnp.int32),
            jax.ShapeDtypeStruct((16,), jnp.int32),
            jax.ShapeDtypeStruct((TAPS, 128), jnp.float32),
        ),
        in_specs=[SMEM, SMEM, SMEM, HBM, HBM, HBM, VMEM],
        out_specs=(VMEM, VMEM, SMEM, VMEM),
        scratch_shapes=[
            pltpu.SMEM((TILES // 4,), jnp.int32),
            pltpu.VMEM(vis.shape, vis.dtype),
            pltpu.VMEM(weight.shape, weight.dtype),
            pltpu.VMEM(pos.shape, pos.dtype),
            pltpu.SemaphoreType.DMA((3,)),
        ],
        compiler_params=pltpu.CompilerParams(vmem_limit_bytes=LIMIT),
        name="sort_blocks",
    )(dest, count, anchor, vis, weight, pos, kernel)


def greet_tiles(me):
    barrier = pltpu.get_barrier_semaphore()

    def greet(step, carry):
        pl.semaphore_signal(
            barrier, inc=1, device_id={"tile": (me + step) % TILES}, device_id_type=MESH
        )
        return carry

    lax.fori_loop(1, TILES, greet, 0)
    return barrier


def route_kernel(scaled, packed, got_scaled, got_packed, s_out, s_in, p_out, p_in, here):
    me = lax.axis_index("tile")
    pl.semaphore_wait(greet_tiles(me), TILES - 1)

    def copies(peer):
        first = pltpu.make_async_remote_copy(
            src_ref=scaled.at[pl.ds(peer * 2, 2)],
            dst_ref=got_scaled.at[pl.ds(me * 2, 2)],
            send_sem=s_out.at[peer],
            recv_sem=s_in.at[me],
            device_id={"tile": peer},
            device_id_type=MESH,
        )
        second = pltpu.make_async_remote_copy(
            src_ref=packed.at[pl.ds(peer, 1)],
            dst_ref=got_packed.at[pl.ds(me, 1)],
            send_sem=p_out.at[peer],
            recv_sem=p_in.at[me],
            device_id={"tile": peer},
            device_id_type=MESH,
        )
        return first, second

    def send(step, carry):
        first, second = copies((me + step) % TILES)
        first.start()
        second.start()
        return carry

    lax.fori_loop(1, TILES, send, 0)
    own_scaled = pltpu.make_async_copy(
        scaled.at[pl.ds(me * 2, 2)], got_scaled.at[pl.ds(me * 2, 2)], here.at[0]
    )
    own_packed = pltpu.make_async_copy(
        packed.at[pl.ds(me, 1)], got_packed.at[pl.ds(me, 1)], here.at[1]
    )
    own_scaled.start()
    own_packed.start()
    own_scaled.wait()
    own_packed.wait()

    def finish(step, carry):
        peer = (me + step) % TILES
        pltpu.make_async_copy(
            got_scaled.at[pl.ds(peer * 2, 2)], got_scaled.at[pl.ds(peer * 2, 2)], s_in.at[peer]
        ).wait()
        pltpu.make_async_copy(
            got_packed.at[pl.ds(peer, 1)], got_packed.at[pl.ds(peer, 1)], p_in.at[peer]
        ).wait()
        first, second = copies(peer)
        first.wait_send()
        second.wait_send()
        return carry

    lax.fori_loop(1, TILES, finish, 0)


def route(scaled, packed):
    return pl.pallas_call(
        route_kernel,
        out_shape=(
            jax.ShapeDtypeStruct(scaled.shape, scaled.dtype),
            jax.ShapeDtypeStruct(packed.shape, packed.dtype),
        ),
        in_specs=[VMEM, VMEM],
        out_specs=(VMEM, VMEM),
        scratch_shapes=[pltpu.SemaphoreType.DMA((TILES,))] * 4 + [pltpu.SemaphoreType.DMA((2,))],
        compiler_params=pltpu.CompilerParams(
            collective_id=0, has_side_effects=True, vmem_limit_bytes=LIMIT
        ),
        name="route",
    )(scaled, packed)


def live_turns(count, one):
    def many(start, width):
        def step(turn, carry):
            for k in range(width):
                at = start + turn * width + k
                one(jnp.where(at < count, at, 0), at < count)
            return carry

        return step

    eights = count >> 3
    lax.fori_loop(0, eights, many(0, 8), 0)
    lax.fori_loop(0, (count - eights * 8 + 1) >> 1, many(eights * 8, 2), 0)


def tap_tiles(table, cell, column, pieces):
    cell = jnp.broadcast_to(cell, (8, 128))
    column = jnp.broadcast_to(column, (8, 128))
    low = jnp.take_along_axis(table[:8], column, axis=1, mode="promise_in_bounds")
    high = jnp.take_along_axis(table[8:], column, axis=1, mode="promise_in_bounds")
    sub = lax.broadcasted_iota(jnp.int32, (8, 128), 0)
    part = cell & 7
    turn = (sub - part) & 7
    low = jnp.take_along_axis(low, turn, axis=0, mode="promise_in_bounds")
    high = jnp.take_along_axis(high, turn, axis=0, mode="promise_in_bounds")
    after = sub >= part
    zero = jnp.zeros((8, 128), jnp.float32)
    first = jnp.where(after, low, zero)
    second = jnp.where(after, high, low)
    third = jnp.where(after, zero, high)
    late = (cell & 8) == 8

    def both(upper, lower):
        return jnp.concatenate([upper, lower], axis=0).astype(jnp.bfloat16)

    begin = both(jnp.where(late, zero, first), jnp.where(late, first, second))
    end = both(jnp.where(late, second, third), jnp.where(late, third, zero))
    whole = (cell >> 4).astype(jnp.float32)
    whole = both(whole, whole)
    blank = jnp.zeros((16, 128), jnp.bfloat16)
    at = [whole == jnp.bfloat16(m) for m in range(pieces)]
    tiles = []
    for m in range(pieces):
        value = jnp.where(at[m - 1], end, blank) if m else blank
        tiles.append(jnp.where(at[m], begin, value))
    return tiles


def slot_taps(packed, table, slot, word):
    both = packed[slot >> 1]
    mine = jnp.where((slot & 1) == 1, both[1:2], both[0:1])
    shift = OS * ((word >> 30) & 1)
    row_cell = (mine >> 5) & 255
    row_column = (mine & (OS - 1)) + shift
    col_cell = (mine >> 18) & 255
    col_column = ((mine >> 13) & (OS - 1)) + shift
    lanes = [slice(g * 128, (g + 1) * 128) for g in range(GROUPS)]
    rows = [tap_tiles(table, row_cell[:, k], row_column[:, k], ROWS // 16) for k in lanes]
    cols = [
        jnp.concatenate(tap_tiles(table, col_cell[:, k], col_column[:, k], TS // 16), axis=0)
        for k in lanes
    ]
    return rows, jnp.concatenate(cols, axis=1)


def grid_kernel(scaled, packed, table, grid, live, words, line, heads, sem):
    flags = jnp.concatenate([packed[:, 0, 0:128], packed[:, 1, 0:128]], axis=0)
    line[...] = jnp.broadcast_to(flags.T[0:1], (8, 128))
    fetch = pltpu.make_async_copy(line, heads, sem)
    fetch.start()
    grid[...] = jnp.zeros(grid.shape, grid.dtype)
    taps = table[...]
    fetch.wait()

    def look(device, count):
        for which in range(2):
            word = heads[0, which * TILES + device]
            live[count] = device * 2 + which
            words[count] = word
            count = count + ((word >> 26) & 1)
        return count

    count = lax.fori_loop(0, TILES, look, jnp.int32(0), unroll=4)
    live[SLOTS] = count

    def one(k, alive):
        slot, word = live[k], words[k]
        rows, cols = slot_taps(packed, taps, slot, word)
        keep = alive.astype(jnp.float32)
        planes = []
        for part in range(2):
            values = scaled[slot, part].astype(jnp.float32) * keep
            for channel in range(2):
                lanes = []
                for g in range(GROUPS):
                    value = values[channel : channel + 1, g * 128 : (g + 1) * 128]
                    value = jnp.broadcast_to(value, (16, 128)).astype(jnp.bfloat16)
                    lanes.append(jnp.concatenate([tile * value for tile in rows[g]], axis=0))
                planes.append(jnp.concatenate(lanes, axis=1))
        product = lax.dot_general(
            jnp.concatenate(planes, axis=0),
            cols,
            (((1,), (1,)), ((), ())),
            preferred_element_type=jnp.float32,
        )
        pair = (word >> 31) & 1
        start = pl.multiple_of(((word >> 27) & 7) * 16, 16)
        for plane in range(4):
            grid[pair, plane, pl.ds(start, ROWS), :] += product[plane * ROWS : (plane + 1) * ROWS]

    live_turns(count, one)


def grid_blocks(scaled, packed, table):
    return pl.pallas_call(
        grid_kernel,
        out_shape=(
            jax.ShapeDtypeStruct((2, 4, TS, TS), jnp.float32),
            jax.ShapeDtypeStruct((SLOTS + 8,), jnp.int32),
            jax.ShapeDtypeStruct((SLOTS + 8,), jnp.int32),
        ),
        in_specs=[VMEM, VMEM, VMEM],
        out_specs=(VMEM, SMEM, SMEM),
        scratch_shapes=[pltpu.VMEM((8, 128), jnp.int32), pltpu.SMEM((8, 128), jnp.int32), pltpu.SemaphoreType.DMA],
        compiler_params=pltpu.CompilerParams(vmem_limit_bytes=LIMIT),
        name="grid_blocks",
    )(scaled, packed, table)


def join_kernel(grid, whole, summed, half, got_half, total, mine, got_mine, send, recv):
    me = lax.axis_index("tile")
    core = me & 1
    near = me ^ 1
    far = me ^ (TILES // 2)
    barrier = pltpu.get_barrier_semaphore()
    for peer in (near, far):
        pl.semaphore_signal(barrier, inc=1, device_id={"tile": peer}, device_id_type=MESH)

    def pass_on(source, target, sem, peer):
        return pltpu.make_async_remote_copy(
            src_ref=source,
            dst_ref=target,
            send_sem=send.at[sem],
            recv_sem=recv.at[sem],
            device_id={"tile": peer},
            device_id_type=MESH,
        )

    pl.semaphore_wait(barrier, 2)
    first = [pass_on(half.at[k], got_half.at[k], k, near) for k in range(4)]
    second = [pass_on(mine.at[k], got_mine.at[k], 4 + k, far) for k in range(4)]
    third = [pass_on(whole.at[core, k], whole.at[core, k], 8 + k, near) for k in range(4)]
    for k in range(4):
        half[k] = grid[1 - core, k].astype(jnp.bfloat16)
        first[k].start()
    for k in range(4):
        first[k].wait_recv()
        value = grid[core, k] + got_half[k].astype(jnp.float32)
        total[k] = value
        mine[k] = value.astype(jnp.bfloat16)
        second[k].start()
    for k in range(4):
        second[k].wait_recv()
        value = total[k] + got_mine[k].astype(jnp.float32)
        whole[core, k] = value.astype(jnp.bfloat16)
        third[k].start()
        if k % 2 == 0:
            summed[k // 2] = value
        else:
            summed[k // 2] += value
    for k in range(4):
        other = pltpu.make_async_copy(whole.at[1 - core, k], whole.at[1 - core, k], recv.at[8 + k])
        other.wait()
        first[k].wait_send()
        second[k].wait_send()
        third[k].wait_send()


def join_grids(grid):
    return pl.pallas_call(
        join_kernel,
        out_shape=(
            jax.ShapeDtypeStruct((2, 4, TS, TS), jnp.bfloat16),
            jax.ShapeDtypeStruct((2, TS, TS), jnp.float32),
        ),
        in_specs=[VMEM],
        out_specs=(VMEM, VMEM),
        scratch_shapes=[
            pltpu.VMEM((4, TS, TS), jnp.bfloat16),
            pltpu.VMEM((4, TS, TS), jnp.bfloat16),
            pltpu.VMEM((4, TS, TS), jnp.float32),
            pltpu.VMEM((4, TS, TS), jnp.bfloat16),
            pltpu.VMEM((4, TS, TS), jnp.bfloat16),
            pltpu.SemaphoreType.DMA((12,)),
            pltpu.SemaphoreType.DMA((12,)),
        ],
        compiler_params=pltpu.CompilerParams(
            collective_id=1, has_side_effects=True, vmem_limit_bytes=LIMIT
        ),
        name="join_grids",
    )(grid)


def turn_over(value):
    sub = lax.broadcasted_iota(jnp.int32, (8, 128), 0)
    lane = lax.broadcasted_iota(jnp.int32, (8, 128), 1)

    def reverse(tile):
        tile = jnp.take_along_axis(tile, 127 - lane, axis=1, mode="promise_in_bounds")
        return jnp.take_along_axis(tile, 7 - sub, axis=0, mode="promise_in_bounds")

    rows = []
    for m in reversed(range(TS // 8)):
        tiles = [reverse(value[m * 8 : m * 8 + 8, k * 128 : k * 128 + 128]) for k in (1, 0)]
        rows.append(jnp.concatenate(tiles, axis=1))
    return jnp.concatenate(rows, axis=0)


def degrid_kernel(live, words, packed, table, whole, summed, predicted, framed):
    upper = lax.axis_index("tile") // (TILES // 2)
    taps = table[...]

    @pl.when(upper == 1)
    def _():
        framed[0] = turn_over(summed[0])
        framed[1] = -turn_over(summed[1])

    @pl.when(upper == 0)
    def _():
        framed[...] = summed[...]

    def one(k, alive):
        slot, word = live[k], words[k]
        rows, cols = slot_taps(packed, taps, slot, word)
        rows = [jnp.concatenate(tiles, axis=0).astype(jnp.float32) for tiles in rows]
        pair = (word >> 31) & 1
        start = pl.multiple_of(((word >> 27) & 7) * 16, 16)
        scale = jnp.float32(1.0 / (TAPS * TAPS))
        for part in range(2):
            results = []
            for channel in range(2):
                window = whole[pair, part * 2 + channel, pl.ds(start, ROWS), :]
                across = jnp.dot(window, cols, preferred_element_type=jnp.float32)
                sums = [
                    jnp.sum(rows[g] * across[:, g * 128 : (g + 1) * 128], axis=0, keepdims=True)
                    for g in range(GROUPS)
                ]
                results.append(jnp.concatenate(sums, axis=1))
            predicted[slot, part] = (jnp.concatenate(results, axis=0) * scale).astype(jnp.bfloat16)

    live_turns(live[SLOTS], one)


def degrid_blocks(live, words, packed, table, whole, summed):
    return pl.pallas_call(
        degrid_kernel,
        out_shape=(
            jax.ShapeDtypeStruct((SLOTS, 2, 2, BLOCK), jnp.bfloat16),
            jax.ShapeDtypeStruct((2, TS, TS), jnp.float32),
        ),
        in_specs=[SMEM, SMEM, VMEM, VMEM, VMEM, VMEM],
        out_specs=(VMEM, VMEM),
        compiler_params=pltpu.CompilerParams(vmem_limit_bytes=LIMIT),
        name="degrid_blocks",
    )(live, words, packed, table, whole, summed)


def back_kernel(
    info, predicted, vis, summed, residual, combined, back, parts, b_out, b_in, c_out, c_in, here
):
    me = lax.axis_index("tile")
    chan = lax.axis_index("chan")
    barrier = greet_tiles(me)
    for k in range(1, CHAN):
        pl.semaphore_signal(
            barrier, inc=1, device_id={"chan": (chan + k) % CHAN}, device_id_type=MESH
        )
    pl.semaphore_wait(barrier, TILES - 1 + CHAN - 1)

    def rows_of(group):
        return pl.ds(pl.multiple_of(group * (TS // CHAN), TS // CHAN), TS // CHAN)

    def across(k):
        group = (chan + k) % CHAN
        return pltpu.make_async_remote_copy(
            src_ref=summed.at[:, rows_of(group), :],
            dst_ref=parts.at[k - 1],
            send_sem=c_out.at[k - 1],
            recv_sem=c_in.at[k - 1],
            device_id={"chan": group},
            device_id_type=MESH,
        )

    def home(peer):
        return pltpu.make_async_remote_copy(
            src_ref=predicted.at[pl.ds(peer * 2, 2)],
            dst_ref=back.at[pl.ds(me * 2, 2)],
            send_sem=b_out.at[peer],
            recv_sem=b_in.at[me],
            device_id={"tile": peer},
            device_id_type=MESH,
        )

    def send(step, carry):
        home((me + step) % TILES).start()
        return carry

    for k in range(1, CHAN):
        across(k).start()
    lax.fori_loop(1, TILES, send, 0)
    own = pltpu.make_async_copy(
        predicted.at[pl.ds(me * 2, 2)], back.at[pl.ds(me * 2, 2)], here.at[0]
    )
    own.start()
    total = summed[:, rows_of(chan), :]
    for k in range(1, CHAN):
        across(k).wait()
        total = total + parts[k - 1]
    combined[...] = total
    own.wait()

    def finish(step, carry):
        peer = (me + step) % TILES
        pltpu.make_async_copy(
            back.at[pl.ds(peer * 2, 2)], back.at[pl.ds(peer * 2, 2)], b_in.at[peer]
        ).wait()
        home(peer).wait_send()
        return carry

    lax.fori_loop(1, TILES, finish, 0)
    for first in range(0, 16, 4):
        results = []
        for b in range(first, first + 4):
            word = info[b]
            keep = ((word >> 9) & 1).astype(jnp.float32)
            flip = (1 - 2 * ((word >> 8) & 1)).astype(jnp.float32)
            for part in range(2):
                value = back[word & 127, part].astype(jnp.float32)
                value = jnp.where(keep > 0.5, value * flip if part else value, jnp.float32(0.0))
                results.append((vis[b, part].astype(jnp.float32) - value).astype(jnp.bfloat16))
        for k, result in enumerate(results):
            residual[first + k // 2, k % 2] = result


def send_back(info, predicted, vis, summed):
    return pl.pallas_call(
        back_kernel,
        out_shape=(
            jax.ShapeDtypeStruct(vis.shape, vis.dtype),
            jax.ShapeDtypeStruct((2, TS // CHAN, TS), jnp.float32),
        ),
        in_specs=[SMEM, VMEM, VMEM, VMEM],
        out_specs=(VMEM, VMEM),
        scratch_shapes=[
            pltpu.VMEM((SLOTS, 2, 2, BLOCK), jnp.bfloat16),
            pltpu.VMEM((CHAN - 1, 2, TS // CHAN, TS), jnp.float32),
            pltpu.SemaphoreType.DMA((TILES,)),
            pltpu.SemaphoreType.DMA((TILES,)),
            pltpu.SemaphoreType.DMA((CHAN - 1,)),
            pltpu.SemaphoreType.DMA((CHAN - 1,)),
            pltpu.SemaphoreType.DMA((1,)),
        ],
        compiler_params=pltpu.CompilerParams(
            collective_id=2, has_side_effects=True, vmem_limit_bytes=LIMIT
        ),
        name="send_back",
    )(info, predicted, vis, summed)


def per_device(visibility, imaging_weight, position, anchor, destination, block_count, kernel):
    scaled, packed, info, table = sort_blocks(
        destination, block_count, anchor.T, visibility, imaging_weight, position, kernel.T
    )
    scaled, packed = route(scaled, packed)
    grid, live, words = grid_blocks(scaled, packed, table)
    whole, summed = join_grids(grid)
    predicted, framed = degrid_blocks(live, words, packed, table, whole, summed)
    residual, combined = send_back(info, predicted, visibility, framed)
    return combined, residual


def solution(mesh):
    placed = (
        P("tile", None, "chan", None),
        P("tile", "chan", None),
        P("tile", None, None),
        P("tile", None),
        P("tile"),
        P("tile"),
        P(),
    )
    return jax.shard_map(
        per_device,
        mesh=mesh,
        in_specs=placed,
        out_specs=(P(None, ("tile", "chan"), None), P("tile", None, "chan", None)),
        check_vma=False,
    )
```

```python
import functools

import jax
import jax.numpy as jnp
from jax import lax
from jax.experimental import pallas as pl
from jax.experimental.pallas import tpu as pltpu
from jax.sharding import PartitionSpec as P

BLOCK = 512
TAPS = 16
OS = 32
SUB = 128
TS = 256
TILES = 64
CHAN = 4
SLOTS = 128
ROWS = 144
GROUPS = 4
LIMIT = 40 * 1024 * 1024

VMEM = pl.BlockSpec(memory_space=pltpu.VMEM)
SMEM = pl.BlockSpec(memory_space=pltpu.SMEM)
HBM = pl.BlockSpec(memory_space=pltpu.HBM)
MESH = pl.DeviceIdType.MESH


def sort_kernel(
    far_dest,
    count,
    far_anchor,
    far_vis,
    far_weight,
    far_pos,
    far_kernel,
    scaled,
    packed,
    info,
    table,
    used,
    dest,
    anchor,
    vis,
    weight,
    pos,
    kernel,
    sems,
):
    fetches = [
        pltpu.make_async_copy(source, target, sems.at[k])
        for k, (source, target) in enumerate(
            (
                (far_dest, dest),
                (far_anchor, anchor),
                (far_vis, vis),
                (far_weight, weight),
                (far_pos, pos),
                (far_kernel, kernel),
            )
        )
    ]
    for fetch in fetches:
        fetch.start()
    me = lax.axis_index("tile")
    turn = me + (me >> 2) + (me >> 4)
    scaled[...] = jnp.zeros(scaled.shape, scaled.dtype)
    packed[...] = jnp.zeros(packed.shape, packed.dtype)
    for quad in range(TILES // 4):
        used[quad] = 0

    def ones_where(mask):
        return jnp.where(mask, jnp.float32(1.0), jnp.float32(0.0)).astype(jnp.bfloat16)

    def iota(shape, axis):
        return lax.broadcasted_iota(jnp.int32, shape, axis)

    fetches[5].wait()
    values = kernel[...].astype(jnp.bfloat16)
    swap = ones_where(iota((TAPS, TAPS), 0) + iota((TAPS, TAPS), 1) == TAPS - 1)
    turned = jnp.dot(swap, values, preferred_element_type=jnp.float32).astype(jnp.bfloat16)
    spread = iota((OS, 128), 1) - iota((OS, 128), 0)
    table[...] = jnp.dot(
        values, ones_where(spread == 0), preferred_element_type=jnp.float32
    ) + jnp.dot(turned, ones_where(spread == OS), preferred_element_type=jnp.float32)
    for fetch in fetches[:5]:
        fetch.wait()
    for b in range(16):
        alive = (b < count[0]).astype(jnp.int32)
        tile = dest[b]
        quad = (tile & 31) >> 1
        rank = used[quad]
        used[quad] = rank + alive
        member = (rank + turn) & 3
        device = (quad << 1) | (member & 1) | ((member >> 1) << 5)
        which = rank >> 2
        mirror = tile >> 5
        flip = 1 - 2 * mirror
        top = mirror * (TS - SUB) + flip * anchor[0, b]
        left = mirror * (TS - SUB) + flip * anchor[1, b]
        base = jnp.minimum(top >> 4, 7)
        info[b] = (device * 2 + which) | (mirror << 8) | (alive << 9)
        meta = (alive << 26) | (base << 27) | (mirror << 30) | ((tile & 1) << 31)

        @pl.when(alive == 1)
        def _():
            place = pos[b]
            cell = mirror * (SUB - TAPS) + flip * (place >> 5)
            offset = place & (OS - 1)
            row = (cell[0:1] + (top - base * 16)) * OS + offset[0:1]
            column = (cell[1:2] + left) * OS + offset[1:2]
            packed[device, pl.ds(which, 1), :] = row | (column << 13) | meta
            factor = weight[b].astype(jnp.float32)
            sign = flip.astype(jnp.float32)
            slot = device * 2 + which
            scaled[slot, 0] = (vis[b, 0].astype(jnp.float32) * factor).astype(jnp.bfloat16)
            scaled[slot, 1] = (vis[b, 1].astype(jnp.float32) * (factor * sign)).astype(jnp.bfloat16)


def in_hbm(array):
    return pltpu.with_memory_space_constraint(array, pltpu.HBM)


def sort_blocks(dest, count, anchor, vis, weight, pos, kernel):
    return pl.pallas_call(
        sort_kernel,
        out_shape=(
            jax.ShapeDtypeStruct((SLOTS, 2, 2, BLOCK), jnp.bfloat16),
            jax.ShapeDtypeStruct((TILES, 2, BLOCK), jnp.int32),
            jax.ShapeDtypeStruct((16,), jnp.int32),
            jax.ShapeDtypeStruct((TAPS, 128), jnp.float32),
        ),
        in_specs=[HBM, SMEM, HBM, HBM, HBM, HBM, HBM],
        out_specs=(VMEM, VMEM, SMEM, VMEM),
        scratch_shapes=[
            pltpu.SMEM((TILES // 4,), jnp.int32),
            pltpu.SMEM(dest.shape, dest.dtype),
            pltpu.SMEM(anchor.shape, anchor.dtype),
            pltpu.VMEM(vis.shape, vis.dtype),
            pltpu.VMEM(weight.shape, weight.dtype),
            pltpu.VMEM(pos.shape, pos.dtype),
            pltpu.VMEM(kernel.shape, kernel.dtype),
            pltpu.SemaphoreType.DMA((6,)),
        ],
        compiler_params=pltpu.CompilerParams(vmem_limit_bytes=LIMIT),
        name="sort_blocks",
    )(in_hbm(dest), count, *map(in_hbm, (anchor, vis, weight, pos, kernel)))


def greet_tiles(me):
    barrier = pltpu.get_barrier_semaphore()

    def greet(step, carry):
        pl.semaphore_signal(
            barrier, inc=1, device_id={"tile": (me + step) % TILES}, device_id_type=MESH
        )
        return carry

    lax.fori_loop(1, TILES, greet, 0)
    return barrier


def route_kernel(scaled, packed, got_scaled, got_packed, sems, here):
    me = lax.axis_index("tile")
    pl.semaphore_wait(greet_tiles(me), TILES - 1)

    def copies(peer):
        first = pltpu.make_async_remote_copy(
            src_ref=scaled.at[pl.ds(peer * 2, 2)],
            dst_ref=got_scaled.at[pl.ds(me * 2, 2)],
            send_sem=sems.at[0],
            recv_sem=sems.at[1],
            device_id={"tile": peer},
            device_id_type=MESH,
        )
        second = pltpu.make_async_remote_copy(
            src_ref=packed.at[pl.ds(peer, 1)],
            dst_ref=got_packed.at[pl.ds(me, 1)],
            send_sem=sems.at[2],
            recv_sem=sems.at[3],
            device_id={"tile": peer},
            device_id_type=MESH,
        )
        return first, second

    def send(step, carry):
        first, second = copies((me + step) % TILES)
        first.start()
        second.start()
        return carry

    lax.fori_loop(1, TILES, send, 0)
    own_scaled = pltpu.make_async_copy(
        scaled.at[pl.ds(me * 2, 2)], got_scaled.at[pl.ds(me * 2, 2)], here.at[0]
    )
    own_packed = pltpu.make_async_copy(
        packed.at[pl.ds(me, 1)], got_packed.at[pl.ds(me, 1)], here.at[1]
    )
    own_scaled.start()
    own_packed.start()
    own_scaled.wait()
    own_packed.wait()

    most_scaled = scaled.at[pl.ds(0, SLOTS - 2)]
    most_packed = packed.at[pl.ds(0, TILES - 1)]
    for k, most in enumerate((most_scaled, most_scaled, most_packed, most_packed)):
        pltpu.make_async_copy(most, most, sems.at[k]).wait()


def route(scaled, packed):
    return pl.pallas_call(
        route_kernel,
        out_shape=(
            jax.ShapeDtypeStruct(scaled.shape, scaled.dtype),
            jax.ShapeDtypeStruct(packed.shape, packed.dtype),
        ),
        in_specs=[VMEM, VMEM],
        out_specs=(VMEM, VMEM),
        scratch_shapes=[pltpu.SemaphoreType.DMA((4,)), pltpu.SemaphoreType.DMA((2,))],
        compiler_params=pltpu.CompilerParams(
            collective_id=0, has_side_effects=True, vmem_limit_bytes=LIMIT
        ),
        name="route",
    )(scaled, packed)


def live_turns(count, one):
    def many(start, width):
        def step(turn, carry):
            for k in range(width):
                at = start + turn * width + k
                one(jnp.where(at < count, at, 0), at < count)
            return carry

        return step

    eights = count >> 3
    lax.fori_loop(0, eights, many(0, 8), 0)
    lax.fori_loop(0, (count - eights * 8 + 1) >> 1, many(eights * 8, 2), 0)


def tap_tiles(table, cell, column, pieces):
    cell = jnp.broadcast_to(cell, (8, 128))
    column = jnp.broadcast_to(column, (8, 128))
    low = jnp.take_along_axis(table[:8], column, axis=1, mode="promise_in_bounds")
    high = jnp.take_along_axis(table[8:], column, axis=1, mode="promise_in_bounds")
    sub = lax.broadcasted_iota(jnp.int32, (8, 128), 0)
    part = cell & 7
    turn = (sub - part) & 7
    low = jnp.take_along_axis(low, turn, axis=0, mode="promise_in_bounds")
    high = jnp.take_along_axis(high, turn, axis=0, mode="promise_in_bounds")
    after = sub >= part
    zero = jnp.zeros((8, 128), jnp.float32)
    first = jnp.where(after, low, zero)
    second = jnp.where(after, high, low)
    third = jnp.where(after, zero, high)
    late = (cell & 8) == 8

    def both(upper, lower):
        return jnp.concatenate([upper, lower], axis=0).astype(jnp.bfloat16)

    begin = both(jnp.where(late, zero, first), jnp.where(late, first, second))
    end = both(jnp.where(late, second, third), jnp.where(late, third, zero))
    whole = (cell >> 4).astype(jnp.float32)
    whole = both(whole, whole)
    blank = jnp.zeros((16, 128), jnp.bfloat16)
    at = [whole == jnp.bfloat16(m) for m in range(pieces)]
    tiles = []
    for m in range(pieces):
        value = jnp.where(at[m - 1], end, blank) if m else blank
        tiles.append(jnp.where(at[m], begin, value))
    return tiles


def slot_taps(packed, table, slot, word):
    both = packed[slot >> 1]
    mine = jnp.where((slot & 1) == 1, both[1:2], both[0:1])
    shift = OS * ((word >> 30) & 1)
    row_cell = (mine >> 5) & 255
    row_column = (mine & (OS - 1)) + shift
    col_cell = (mine >> 18) & 255
    col_column = ((mine >> 13) & (OS - 1)) + shift
    lanes = [slice(g * 128, (g + 1) * 128) for g in range(GROUPS)]
    rows = [tap_tiles(table, row_cell[:, k], row_column[:, k], ROWS // 16) for k in lanes]
    cols = [
        jnp.concatenate(tap_tiles(table, col_cell[:, k], col_column[:, k], TS // 16), axis=0)
        for k in lanes
    ]
    return rows, jnp.concatenate(cols, axis=1)


def grid_kernel(scaled, packed, table, grid, live, words, line, heads, sem):
    flags = jnp.concatenate([packed[:, 0, 0:128], packed[:, 1, 0:128]], axis=0)
    line[...] = jnp.broadcast_to(flags.T[0:1], (8, 128))
    fetch = pltpu.make_async_copy(line, heads, sem)
    fetch.start()
    grid[...] = jnp.zeros(grid.shape, grid.dtype)
    taps = table[...]
    fetch.wait()

    def look(device, count):
        for which in range(2):
            word = heads[0, which * TILES + device]
            live[count] = device * 2 + which
            words[count] = word
            count = count + ((word >> 26) & 1)
        return count

    count = lax.fori_loop(0, TILES, look, jnp.int32(0), unroll=4)
    live[SLOTS] = count

    def one(k, alive):
        slot, word = live[k], words[k]
        rows, cols = slot_taps(packed, taps, slot, word)
        keep = alive.astype(jnp.float32)
        planes = []
        for part in range(2):
            values = scaled[slot, part].astype(jnp.float32) * keep
            for channel in range(2):
                lanes = []
                for g in range(GROUPS):
                    value = values[channel : channel + 1, g * 128 : (g + 1) * 128]
                    value = jnp.broadcast_to(value, (16, 128)).astype(jnp.bfloat16)
                    lanes.append(jnp.concatenate([tile * value for tile in rows[g]], axis=0))
                planes.append(jnp.concatenate(lanes, axis=1))
        product = lax.dot_general(
            jnp.concatenate(planes, axis=0),
            cols,
            (((1,), (1,)), ((), ())),
            preferred_element_type=jnp.float32,
        )
        pair = (word >> 31) & 1
        start = pl.multiple_of(((word >> 27) & 7) * 16, 16)
        for plane in range(4):
            grid[pair, plane, pl.ds(start, ROWS), :] += product[plane * ROWS : (plane + 1) * ROWS]

    live_turns(count, one)


def grid_blocks(scaled, packed, table):
    return pl.pallas_call(
        grid_kernel,
        out_shape=(
            jax.ShapeDtypeStruct((2, 4, TS, TS), jnp.float32),
            jax.ShapeDtypeStruct((SLOTS + 8,), jnp.int32),
            jax.ShapeDtypeStruct((SLOTS + 8,), jnp.int32),
        ),
        in_specs=[VMEM, VMEM, VMEM],
        out_specs=(VMEM, SMEM, SMEM),
        scratch_shapes=[pltpu.VMEM((8, 128), jnp.int32), pltpu.SMEM((8, 128), jnp.int32), pltpu.SemaphoreType.DMA],
        compiler_params=pltpu.CompilerParams(vmem_limit_bytes=LIMIT),
        name="grid_blocks",
    )(scaled, packed, table)


def join_kernel(grid, whole, summed, half, got_half, total, mine, got_mine, send, recv):
    me = lax.axis_index("tile")
    core = me & 1
    near = me ^ 1
    far = me ^ (TILES // 2)
    barrier = pltpu.get_barrier_semaphore()
    for peer in (near, far):
        pl.semaphore_signal(barrier, inc=1, device_id={"tile": peer}, device_id_type=MESH)

    def pass_on(source, target, sem, peer):
        return pltpu.make_async_remote_copy(
            src_ref=source,
            dst_ref=target,
            send_sem=send.at[sem],
            recv_sem=recv.at[sem],
            device_id={"tile": peer},
            device_id_type=MESH,
        )

    pl.semaphore_wait(barrier, 2)
    first = [pass_on(half.at[k], got_half.at[k], k, near) for k in range(4)]
    second = [pass_on(mine.at[k], got_mine.at[k], 4 + k, far) for k in range(4)]
    third = [pass_on(whole.at[core, k], whole.at[core, k], 8 + k, near) for k in range(4)]
    for k in range(4):
        half[k] = grid[1 - core, k].astype(jnp.bfloat16)
        first[k].start()
    for k in range(4):
        first[k].wait_recv()
        value = grid[core, k] + got_half[k].astype(jnp.float32)
        total[k] = value
        mine[k] = value.astype(jnp.bfloat16)
        second[k].start()
    for k in range(4):
        second[k].wait_recv()
        value = total[k] + got_mine[k].astype(jnp.float32)
        whole[core, k] = value.astype(jnp.bfloat16)
        third[k].start()
        if k % 2 == 0:
            summed[k // 2] = value
        else:
            summed[k // 2] += value
    for k in range(4):
        other = pltpu.make_async_copy(whole.at[1 - core, k], whole.at[1 - core, k], recv.at[8 + k])
        other.wait()
        first[k].wait_send()
        second[k].wait_send()
        third[k].wait_send()


def join_grids(grid):
    return pl.pallas_call(
        join_kernel,
        out_shape=(
            jax.ShapeDtypeStruct((2, 4, TS, TS), jnp.bfloat16),
            jax.ShapeDtypeStruct((2, TS, TS), jnp.float32),
        ),
        in_specs=[VMEM],
        out_specs=(VMEM, VMEM),
        scratch_shapes=[
            pltpu.VMEM((4, TS, TS), jnp.bfloat16),
            pltpu.VMEM((4, TS, TS), jnp.bfloat16),
            pltpu.VMEM((4, TS, TS), jnp.float32),
            pltpu.VMEM((4, TS, TS), jnp.bfloat16),
            pltpu.VMEM((4, TS, TS), jnp.bfloat16),
            pltpu.SemaphoreType.DMA((12,)),
            pltpu.SemaphoreType.DMA((12,)),
        ],
        compiler_params=pltpu.CompilerParams(
            collective_id=1, has_side_effects=True, vmem_limit_bytes=LIMIT
        ),
        name="join_grids",
    )(grid)


def turn_over(value):
    sub = lax.broadcasted_iota(jnp.int32, (8, 128), 0)
    lane = lax.broadcasted_iota(jnp.int32, (8, 128), 1)

    def reverse(tile):
        tile = jnp.take_along_axis(tile, 127 - lane, axis=1, mode="promise_in_bounds")
        return jnp.take_along_axis(tile, 7 - sub, axis=0, mode="promise_in_bounds")

    rows = []
    for m in reversed(range(TS // 8)):
        tiles = [reverse(value[m * 8 : m * 8 + 8, k * 128 : k * 128 + 128]) for k in (1, 0)]
        rows.append(jnp.concatenate(tiles, axis=1))
    return jnp.concatenate(rows, axis=0)


def degrid_kernel(live, words, packed, table, whole, summed, predicted, framed):
    upper = lax.axis_index("tile") // (TILES // 2)
    taps = table[...]

    @pl.when(upper == 1)
    def _():
        framed[0] = turn_over(summed[0])
        framed[1] = -turn_over(summed[1])

    @pl.when(upper == 0)
    def _():
        framed[...] = summed[...]

    def one(k, alive):
        slot, word = live[k], words[k]
        rows, cols = slot_taps(packed, taps, slot, word)
        rows = [jnp.concatenate(tiles, axis=0).astype(jnp.float32) for tiles in rows]
        pair = (word >> 31) & 1
        start = pl.multiple_of(((word >> 27) & 7) * 16, 16)
        scale = jnp.float32(1.0 / (TAPS * TAPS))
        for part in range(2):
            results = []
            for channel in range(2):
                window = whole[pair, part * 2 + channel, pl.ds(start, ROWS), :]
                across = jnp.dot(window, cols, preferred_element_type=jnp.float32)
                sums = [
                    jnp.sum(rows[g] * across[:, g * 128 : (g + 1) * 128], axis=0, keepdims=True)
                    for g in range(GROUPS)
                ]
                results.append(jnp.concatenate(sums, axis=1))
            predicted[slot, part] = (jnp.concatenate(results, axis=0) * scale).astype(jnp.bfloat16)

    live_turns(live[SLOTS], one)


def degrid_blocks(live, words, packed, table, whole, summed):
    return pl.pallas_call(
        degrid_kernel,
        out_shape=(
            jax.ShapeDtypeStruct((SLOTS, 2, 2, BLOCK), jnp.bfloat16),
            jax.ShapeDtypeStruct((2, TS, TS), jnp.float32),
        ),
        in_specs=[SMEM, SMEM, VMEM, VMEM, VMEM, VMEM],
        out_specs=(VMEM, VMEM),
        compiler_params=pltpu.CompilerParams(vmem_limit_bytes=LIMIT),
        name="degrid_blocks",
    )(live, words, packed, table, whole, summed)


def back_kernel(
    info, predicted, vis, summed, residual, combined, back, parts, b_sems, c_out, c_in, here
):
    me = lax.axis_index("tile")
    chan = lax.axis_index("chan")
    barrier = greet_tiles(me)
    for k in range(1, CHAN):
        pl.semaphore_signal(
            barrier, inc=1, device_id={"chan": (chan + k) % CHAN}, device_id_type=MESH
        )
    pl.semaphore_wait(barrier, TILES - 1 + CHAN - 1)

    def rows_of(group):
        return pl.ds(pl.multiple_of(group * (TS // CHAN), TS // CHAN), TS // CHAN)

    def across(k):
        group = (chan + k) % CHAN
        return pltpu.make_async_remote_copy(
            src_ref=summed.at[:, rows_of(group), :],
            dst_ref=parts.at[k - 1],
            send_sem=c_out.at[k - 1],
            recv_sem=c_in.at[k - 1],
            device_id={"chan": group},
            device_id_type=MESH,
        )

    def home(peer):
        return pltpu.make_async_remote_copy(
            src_ref=predicted.at[pl.ds(peer * 2, 2)],
            dst_ref=back.at[pl.ds(me * 2, 2)],
            send_sem=b_sems.at[0],
            recv_sem=b_sems.at[1],
            device_id={"tile": peer},
            device_id_type=MESH,
        )

    def send(step, carry):
        home((me + step) % TILES).start()
        return carry

    lax.fori_loop(1, TILES, send, 0)
    for k in range(1, CHAN):
        across(k).start()
    own = pltpu.make_async_copy(
        predicted.at[pl.ds(me * 2, 2)], back.at[pl.ds(me * 2, 2)], here.at[0]
    )
    own.start()
    total = summed[:, rows_of(chan), :]
    for k in range(1, CHAN):
        across(k).wait()
        total = total + parts[k - 1]
    combined[...] = total
    own.wait()

    most = predicted.at[pl.ds(0, SLOTS - 2)]
    for k in range(2):
        pltpu.make_async_copy(most, most, b_sems.at[k]).wait()
    for first in range(0, 16, 4):
        results = []
        for b in range(first, first + 4):
            word = info[b]
            keep = ((word >> 9) & 1).astype(jnp.float32)
            flip = (1 - 2 * ((word >> 8) & 1)).astype(jnp.float32)
            for part in range(2):
                value = back[word & 127, part].astype(jnp.float32)
                value = jnp.where(keep > 0.5, value * flip if part else value, jnp.float32(0.0))
                results.append((vis[b, part].astype(jnp.float32) - value).astype(jnp.bfloat16))
        for k, result in enumerate(results):
            residual[first + k // 2, k % 2] = result


def send_back(info, predicted, vis, summed):
    return pl.pallas_call(
        back_kernel,
        out_shape=(
            jax.ShapeDtypeStruct(vis.shape, vis.dtype),
            jax.ShapeDtypeStruct((2, TS // CHAN, TS), jnp.float32),
        ),
        in_specs=[SMEM, VMEM, VMEM, VMEM],
        out_specs=(VMEM, VMEM),
        scratch_shapes=[
            pltpu.VMEM((SLOTS, 2, 2, BLOCK), jnp.bfloat16),
            pltpu.VMEM((CHAN - 1, 2, TS // CHAN, TS), jnp.float32),
            pltpu.SemaphoreType.DMA((2,)),
            pltpu.SemaphoreType.DMA((CHAN - 1,)),
            pltpu.SemaphoreType.DMA((CHAN - 1,)),
            pltpu.SemaphoreType.DMA((1,)),
        ],
        compiler_params=pltpu.CompilerParams(
            collective_id=2, has_side_effects=True, vmem_limit_bytes=LIMIT
        ),
        name="send_back",
    )(info, predicted, vis, summed)


def per_device(visibility, imaging_weight, position, anchor, destination, block_count, kernel):
    scaled, packed, info, table = sort_blocks(
        destination, block_count, anchor.T, visibility, imaging_weight, position, kernel.T
    )
    scaled, packed = route(scaled, packed)
    grid, live, words = grid_blocks(scaled, packed, table)
    whole, summed = join_grids(grid)
    predicted, framed = degrid_blocks(live, words, packed, table, whole, summed)
    residual, combined = send_back(info, predicted, visibility, framed)
    return combined, residual


def solution(mesh):
    placed = (
        P("tile", None, "chan", None),
        P("tile", "chan", None),
        P("tile", None, None),
        P("tile", None),
        P("tile"),
        P("tile"),
        P(),
    )
    return jax.shard_map(
        per_device,
        mesh=mesh,
        in_specs=placed,
        out_specs=(P(None, ("tile", "chan"), None), P("tile", None, "chan", None)),
        check_vma=False,
    )
```

```python
import functools

import jax
import jax.numpy as jnp
from jax import lax
from jax.experimental import pallas as pl
from jax.experimental.pallas import tpu as pltpu
from jax.sharding import PartitionSpec as P

BLOCK = 512
TAPS = 16
OS = 32
SUB = 128
TS = 256
TILES = 64
CHAN = 4
SLOTS = 128
ROWS = 144
GROUPS = 4
WIDTH = 8
LIMIT = 40 * 1024 * 1024

VMEM = pl.BlockSpec(memory_space=pltpu.VMEM)
SMEM = pl.BlockSpec(memory_space=pltpu.SMEM)
HBM = pl.BlockSpec(memory_space=pltpu.HBM)
MESH = pl.DeviceIdType.MESH


def sort_kernel(
    far_dest,
    count,
    far_anchor,
    far_vis,
    far_weight,
    far_pos,
    far_kernel,
    scaled,
    packed,
    info,
    table,
    used,
    dest,
    anchor,
    vis,
    weight,
    pos,
    kernel,
    sems,
):
    fetches = [
        pltpu.make_async_copy(source, target, sems.at[k])
        for k, (source, target) in enumerate(
            (
                (far_dest, dest),
                (far_anchor, anchor),
                (far_vis, vis),
                (far_weight, weight),
                (far_pos, pos),
                (far_kernel, kernel),
            )
        )
    ]
    for fetch in fetches:
        fetch.start()
    me = lax.axis_index("tile")
    turn = me + (me >> 2) + (me >> 4)
    scaled[...] = jnp.zeros(scaled.shape, scaled.dtype)
    packed[...] = jnp.zeros(packed.shape, packed.dtype)
    for quad in range(TILES // 4):
        used[quad] = 0

    def ones_where(mask):
        return jnp.where(mask, jnp.float32(1.0), jnp.float32(0.0)).astype(jnp.bfloat16)

    def iota(shape, axis):
        return lax.broadcasted_iota(jnp.int32, shape, axis)

    fetches[5].wait()
    values = kernel[...].astype(jnp.bfloat16)
    swap = ones_where(iota((TAPS, TAPS), 0) + iota((TAPS, TAPS), 1) == TAPS - 1)
    turned = jnp.dot(swap, values, preferred_element_type=jnp.float32).astype(jnp.bfloat16)
    spread = iota((OS, 128), 1) - iota((OS, 128), 0)
    table[...] = jnp.dot(
        values, ones_where(spread == 0), preferred_element_type=jnp.float32
    ) + jnp.dot(turned, ones_where(spread == OS), preferred_element_type=jnp.float32)
    for fetch in fetches[:5]:
        fetch.wait()
    for b in range(16):
        alive = (b < count[0]).astype(jnp.int32)
        tile = dest[b]
        quad = (tile & 31) >> 1
        rank = used[quad]
        used[quad] = rank + alive
        member = (rank + turn) & 3
        device = (quad << 1) | (member & 1) | ((member >> 1) << 5)
        which = rank >> 2
        mirror = tile >> 5
        flip = 1 - 2 * mirror
        top = mirror * (TS - SUB) + flip * anchor[0, b]
        left = mirror * (TS - SUB) + flip * anchor[1, b]
        base = jnp.minimum(top >> 4, 7)
        info[b] = (device * 2 + which) | (mirror << 8) | (alive << 9)
        meta = (alive << 26) | (base << 27) | (mirror << 30) | ((tile & 1) << 31)

        @pl.when(alive == 1)
        def _():
            place = pos[b]
            cell = mirror * (SUB - TAPS) + flip * (place >> 5)
            offset = place & (OS - 1)
            row = (cell[0:1] + (top - base * 16)) * OS + offset[0:1]
            column = (cell[1:2] + left) * OS + offset[1:2]
            packed[device, pl.ds(which, 1), :] = row | (column << 13) | meta
            factor = weight[b].astype(jnp.float32)
            sign = flip.astype(jnp.float32)
            slot = device * 2 + which
            scaled[slot, 0] = (vis[b, 0].astype(jnp.float32) * factor).astype(jnp.bfloat16)
            scaled[slot, 1] = (vis[b, 1].astype(jnp.float32) * (factor * sign)).astype(jnp.bfloat16)


def in_hbm(array):
    return pltpu.with_memory_space_constraint(array, pltpu.HBM)


def sort_blocks(dest, count, anchor, vis, weight, pos, kernel):
    return pl.pallas_call(
        sort_kernel,
        out_shape=(
            jax.ShapeDtypeStruct((SLOTS, 2, 2, BLOCK), jnp.bfloat16),
            jax.ShapeDtypeStruct((TILES, 2, BLOCK), jnp.int32),
            jax.ShapeDtypeStruct((16,), jnp.int32),
            jax.ShapeDtypeStruct((TAPS, 128), jnp.float32),
        ),
        in_specs=[HBM, SMEM, HBM, HBM, HBM, HBM, HBM],
        out_specs=(VMEM, VMEM, SMEM, VMEM),
        scratch_shapes=[
            pltpu.SMEM((TILES // 4,), jnp.int32),
            pltpu.SMEM(dest.shape, dest.dtype),
            pltpu.SMEM(anchor.shape, anchor.dtype),
            pltpu.VMEM(vis.shape, vis.dtype),
            pltpu.VMEM(weight.shape, weight.dtype),
            pltpu.VMEM(pos.shape, pos.dtype),
            pltpu.VMEM(kernel.shape, kernel.dtype),
            pltpu.SemaphoreType.DMA((6,)),
        ],
        compiler_params=pltpu.CompilerParams(vmem_limit_bytes=LIMIT),
        name="sort_blocks",
    )(in_hbm(dest), count, *map(in_hbm, (anchor, vis, weight, pos, kernel)))


def greet_tiles(me):
    barrier = pltpu.get_barrier_semaphore()

    def greet(step, carry):
        pl.semaphore_signal(
            barrier, inc=1, device_id={"tile": (me + step) % TILES}, device_id_type=MESH
        )
        return carry

    lax.fori_loop(1, TILES, greet, 0)
    return barrier


def route_kernel(scaled, packed, got_scaled, got_packed, sems, here):
    me = lax.axis_index("tile")
    pl.semaphore_wait(greet_tiles(me), TILES - 1)

    def copies(peer):
        first = pltpu.make_async_remote_copy(
            src_ref=scaled.at[pl.ds(peer * 2, 2)],
            dst_ref=got_scaled.at[pl.ds(me * 2, 2)],
            send_sem=sems.at[0],
            recv_sem=sems.at[1],
            device_id={"tile": peer},
            device_id_type=MESH,
        )
        second = pltpu.make_async_remote_copy(
            src_ref=packed.at[pl.ds(peer, 1)],
            dst_ref=got_packed.at[pl.ds(me, 1)],
            send_sem=sems.at[2],
            recv_sem=sems.at[3],
            device_id={"tile": peer},
            device_id_type=MESH,
        )
        return first, second

    def send(step, carry):
        first, second = copies((me + step) % TILES)
        first.start()
        second.start()
        return carry

    lax.fori_loop(1, TILES, send, 0)
    own_scaled = pltpu.make_async_copy(
        scaled.at[pl.ds(me * 2, 2)], got_scaled.at[pl.ds(me * 2, 2)], here.at[0]
    )
    own_packed = pltpu.make_async_copy(
        packed.at[pl.ds(me, 1)], got_packed.at[pl.ds(me, 1)], here.at[1]
    )
    own_scaled.start()
    own_packed.start()
    own_scaled.wait()
    own_packed.wait()

    most_scaled = scaled.at[pl.ds(0, SLOTS - 2)]
    most_packed = packed.at[pl.ds(0, TILES - 1)]
    for k, most in enumerate((most_scaled, most_scaled, most_packed, most_packed)):
        pltpu.make_async_copy(most, most, sems.at[k]).wait()


def route(scaled, packed):
    return pl.pallas_call(
        route_kernel,
        out_shape=(
            jax.ShapeDtypeStruct(scaled.shape, scaled.dtype),
            jax.ShapeDtypeStruct(packed.shape, packed.dtype),
        ),
        in_specs=[VMEM, VMEM],
        out_specs=(VMEM, VMEM),
        scratch_shapes=[pltpu.SemaphoreType.DMA((4,)), pltpu.SemaphoreType.DMA((2,))],
        compiler_params=pltpu.CompilerParams(
            collective_id=0, has_side_effects=True, vmem_limit_bytes=LIMIT
        ),
        name="route",
    )(scaled, packed)


def live_turns(count, one):
    def many(start, width):
        def step(turn, carry):
            for k in range(width):
                at = start + turn * width + k
                one(jnp.where(at < count, at, 0), at < count)
            return carry

        return step

    eights = count >> 3
    lax.fori_loop(0, eights, many(0, 8), 0)
    lax.fori_loop(0, (count - eights * 8 + 1) >> 1, many(eights * 8, 2), 0)


def tap_tiles(table, cell, column, pieces):
    cell = jnp.broadcast_to(cell, (8, 128))
    column = jnp.broadcast_to(column, (8, 128))
    low = jnp.take_along_axis(table[:8], column, axis=1, mode="promise_in_bounds")
    high = jnp.take_along_axis(table[8:], column, axis=1, mode="promise_in_bounds")
    sub = lax.broadcasted_iota(jnp.int32, (8, 128), 0)
    part = cell & 7
    turn = (sub - part) & 7
    low = jnp.take_along_axis(low, turn, axis=0, mode="promise_in_bounds")
    high = jnp.take_along_axis(high, turn, axis=0, mode="promise_in_bounds")
    after = sub >= part
    zero = jnp.zeros((8, 128), jnp.float32)
    first = jnp.where(after, low, zero)
    second = jnp.where(after, high, low)
    third = jnp.where(after, zero, high)
    late = (cell & 8) == 8

    def both(upper, lower):
        return jnp.concatenate([upper, lower], axis=0).astype(jnp.bfloat16)

    begin = both(jnp.where(late, zero, first), jnp.where(late, first, second))
    end = both(jnp.where(late, second, third), jnp.where(late, third, zero))
    whole = (cell >> 4).astype(jnp.float32)
    whole = both(whole, whole)
    blank = jnp.zeros((16, 128), jnp.bfloat16)
    at = [whole == jnp.bfloat16(m) for m in range(pieces)]
    tiles = []
    for m in range(pieces):
        value = jnp.where(at[m - 1], end, blank) if m else blank
        tiles.append(jnp.where(at[m], begin, value))
    return tiles


def slot_taps(packed, table, slot, word):
    both = packed[slot >> 1]
    mine = jnp.where((slot & 1) == 1, both[1:2], both[0:1])
    return word_taps(mine, table, word)


def word_taps(mine, table, word):
    shift = OS * ((word >> 30) & 1)
    row_cell = (mine >> 5) & 255
    row_column = (mine & (OS - 1)) + shift
    col_cell = (mine >> 18) & 255
    col_column = ((mine >> 13) & (OS - 1)) + shift
    lanes = [slice(g * 128, (g + 1) * 128) for g in range(GROUPS)]
    rows = [tap_tiles(table, row_cell[:, k], row_column[:, k], ROWS // 16) for k in lanes]
    cols = [
        jnp.concatenate(tap_tiles(table, col_cell[:, k], col_column[:, k], TS // 16), axis=0)
        for k in lanes
    ]
    return rows, jnp.concatenate(cols, axis=1)


def grid_kernel(scaled, packed, table, grid, heads, late, line, live, sem):
    flags = jnp.concatenate([packed[:, 0, 0:128], packed[:, 1, 0:128]], axis=0)
    line[...] = jnp.broadcast_to(flags.T[0:1], (8, 128))
    fetch = pltpu.make_async_copy(line, heads, sem)
    fetch.start()
    grid[...] = jnp.zeros(grid.shape, grid.dtype)
    taps = table[...]
    fetch.wait()

    def look(device, count):
        live[count] = device * 2
        return count + ((heads[0, device] >> 26) & 1)

    def look_late(device, counts):
        count, extra = counts
        live[count] = device * 2 + 1
        late[extra] = device
        alive = (heads[0, TILES + device] >> 26) & 1
        return count + alive, extra + alive

    count = lax.fori_loop(0, TILES, look, jnp.int32(0), unroll=4)
    count, extra = lax.fori_loop(0, TILES, look_late, (count, jnp.int32(0)), unroll=4)
    late[TILES] = extra

    def one(k, alive):
        slot = live[k]
        word = heads[0, (slot & 1) * TILES + (slot >> 1)]
        rows, cols = slot_taps(packed, taps, slot, word)
        keep = alive.astype(jnp.float32)
        planes = []
        for part in range(2):
            values = scaled[slot, part].astype(jnp.float32) * keep
            for channel in range(2):
                lanes = []
                for g in range(GROUPS):
                    value = values[channel : channel + 1, g * 128 : (g + 1) * 128]
                    value = jnp.broadcast_to(value, (16, 128)).astype(jnp.bfloat16)
                    lanes.append(jnp.concatenate([tile * value for tile in rows[g]], axis=0))
                planes.append(jnp.concatenate(lanes, axis=1))
        product = lax.dot_general(
            jnp.concatenate(planes, axis=0),
            cols,
            (((1,), (1,)), ((), ())),
            preferred_element_type=jnp.float32,
        )
        pair = (word >> 31) & 1
        start = pl.multiple_of(((word >> 27) & 7) * 16, 16)
        for plane in range(4):
            grid[pair, plane, pl.ds(start, ROWS), :] += product[plane * ROWS : (plane + 1) * ROWS]

    live_turns(count, one)


def grid_blocks(scaled, packed, table):
    return pl.pallas_call(
        grid_kernel,
        out_shape=(
            jax.ShapeDtypeStruct((2, 4, TS, TS), jnp.float32),
            jax.ShapeDtypeStruct((8, 128), jnp.int32),
            jax.ShapeDtypeStruct((TILES + 8,), jnp.int32),
        ),
        in_specs=[VMEM, VMEM, VMEM],
        out_specs=(VMEM, SMEM, SMEM),
        scratch_shapes=[
            pltpu.VMEM((8, 128), jnp.int32),
            pltpu.SMEM((SLOTS + 8,), jnp.int32),
            pltpu.SemaphoreType.DMA,
        ],
        compiler_params=pltpu.CompilerParams(vmem_limit_bytes=LIMIT),
        name="grid_blocks",
    )(scaled, packed, table)


def join_kernel(grid, whole, summed, half, got_half, total, mine, got_mine, send, recv):
    me = lax.axis_index("tile")
    core = me & 1
    near = me ^ 1
    far = me ^ (TILES // 2)
    barrier = pltpu.get_barrier_semaphore()
    for peer in (near, far):
        pl.semaphore_signal(barrier, inc=1, device_id={"tile": peer}, device_id_type=MESH)

    def pass_on(source, target, sem, peer):
        return pltpu.make_async_remote_copy(
            src_ref=source,
            dst_ref=target,
            send_sem=send.at[sem],
            recv_sem=recv.at[sem],
            device_id={"tile": peer},
            device_id_type=MESH,
        )

    pl.semaphore_wait(barrier, 2)
    first = [pass_on(half.at[k], got_half.at[k], k, near) for k in range(4)]
    second = [pass_on(mine.at[k], got_mine.at[k], 4 + k, far) for k in range(4)]
    third = [pass_on(whole.at[core, k], whole.at[core, k], 8 + k, near) for k in range(4)]
    for k in range(4):
        half[k] = grid[1 - core, k].astype(jnp.bfloat16)
        first[k].start()
    for k in range(4):
        first[k].wait_recv()
        value = grid[core, k] + got_half[k].astype(jnp.float32)
        total[k] = value
        mine[k] = value.astype(jnp.bfloat16)
        second[k].start()
    for k in range(4):
        second[k].wait_recv()
        value = total[k] + got_mine[k].astype(jnp.float32)
        whole[core, k] = value.astype(jnp.bfloat16)
        third[k].start()
        if k % 2 == 0:
            summed[k // 2] = value
        else:
            summed[k // 2] += value
    for k in range(4):
        other = pltpu.make_async_copy(whole.at[1 - core, k], whole.at[1 - core, k], recv.at[8 + k])
        other.wait()
        first[k].wait_send()
        second[k].wait_send()
        third[k].wait_send()


def join_grids(grid):
    return pl.pallas_call(
        join_kernel,
        out_shape=(
            jax.ShapeDtypeStruct((2, 4, TS, TS), jnp.bfloat16),
            jax.ShapeDtypeStruct((2, TS, TS), jnp.float32),
        ),
        in_specs=[VMEM],
        out_specs=(VMEM, VMEM),
        scratch_shapes=[
            pltpu.VMEM((4, TS, TS), jnp.bfloat16),
            pltpu.VMEM((4, TS, TS), jnp.bfloat16),
            pltpu.VMEM((4, TS, TS), jnp.float32),
            pltpu.VMEM((4, TS, TS), jnp.bfloat16),
            pltpu.VMEM((4, TS, TS), jnp.bfloat16),
            pltpu.SemaphoreType.DMA((12,)),
            pltpu.SemaphoreType.DMA((12,)),
        ],
        compiler_params=pltpu.CompilerParams(
            collective_id=1, has_side_effects=True, vmem_limit_bytes=LIMIT
        ),
        name="join_grids",
    )(grid)


def turn_over(value):
    sub = lax.broadcasted_iota(jnp.int32, (8, 128), 0)
    lane = lax.broadcasted_iota(jnp.int32, (8, 128), 1)

    def reverse(tile):
        tile = jnp.take_along_axis(tile, 127 - lane, axis=1, mode="promise_in_bounds")
        return jnp.take_along_axis(tile, 7 - sub, axis=0, mode="promise_in_bounds")

    rows = []
    for m in reversed(range(TS // 8)):
        tiles = [reverse(value[m * 8 : m * 8 + 8, k * 128 : k * 128 + 128]) for k in (1, 0)]
        rows.append(jnp.concatenate(tiles, axis=1))
    return jnp.concatenate(rows, axis=0)


def predict(whole, rows, cols, word):
    rows = [jnp.concatenate(tiles, axis=0).astype(jnp.float32) for tiles in rows]
    pair = (word >> 31) & 1
    base = (word >> 27) & 7
    scale = jnp.float32(1.0 / (TAPS * TAPS))
    parts = []
    for part in range(2):
        results = []
        for channel in range(2):
            plane = part * 2 + channel
            window = jnp.concatenate(
                [whole[pair, plane, base + k] for k in range(ROWS // 16)], axis=0
            )
            across = jnp.dot(window, cols, preferred_element_type=jnp.float32)
            sums = [
                jnp.sum(rows[g] * across[:, g * 128 : (g + 1) * 128], axis=0, keepdims=True)
                for g in range(GROUPS)
            ]
            results.append(jnp.concatenate(sums, axis=1))
        parts.append((jnp.concatenate(results, axis=0) * scale).astype(jnp.bfloat16))
    return parts


def late_kernel(late, heads, packed, table, whole, summed, predicted, framed):
    upper = lax.axis_index("tile") // (TILES // 2)
    taps = table[...]

    @pl.when(upper == 1)
    def _():
        framed[0] = turn_over(summed[0])
        framed[1] = -turn_over(summed[1])

    @pl.when(upper == 0)
    def _():
        framed[...] = summed[...]

    predicted[...] = jnp.zeros(predicted.shape, predicted.dtype)

    def one(k, carry):
        device = late[k]
        word = heads[0, TILES + device]
        rows, cols = slot_taps(packed, taps, device * 2 + 1, word)
        for part, value in enumerate(predict(whole, rows, cols, word)):
            predicted[device, part] = value
        return carry

    lax.fori_loop(0, late[TILES], one, 0)


def degrid_late(late, heads, packed, table, whole, summed):
    return pl.pallas_call(
        late_kernel,
        out_shape=(
            jax.ShapeDtypeStruct((TILES, 2, 2, BLOCK), jnp.bfloat16),
            jax.ShapeDtypeStruct((2, TS, TS), jnp.float32),
        ),
        in_specs=[SMEM, SMEM, VMEM, VMEM, VMEM, VMEM],
        out_specs=(VMEM, VMEM),
        compiler_params=pltpu.CompilerParams(vmem_limit_bytes=LIMIT),
        name="degrid_late",
    )(late, heads, packed, table, whole, summed)


def back_kernel(
    info,
    heads,
    late,
    packed,
    table,
    whole,
    vis,
    summed,
    residual,
    combined,
    ready,
    back,
    parts,
    b_sems,
    c_out,
    c_in,
):
    me = lax.axis_index("tile")
    chan = lax.axis_index("chan")
    barrier = greet_tiles(me)
    for k in range(1, CHAN):
        pl.semaphore_signal(
            barrier, inc=1, device_id={"chan": (chan + k) % CHAN}, device_id_type=MESH
        )
    taps = table[...]

    def rows_of(group):
        return pl.ds(pl.multiple_of(group * (TS // CHAN), TS // CHAN), TS // CHAN)

    def across(k):
        group = (chan + k) % CHAN
        return pltpu.make_async_remote_copy(
            src_ref=summed.at[:, rows_of(group), :],
            dst_ref=parts.at[k - 1],
            send_sem=c_out.at[k - 1],
            recv_sem=c_in.at[k - 1],
            device_id={"chan": group},
            device_id_type=MESH,
        )

    def make(peer):
        word = heads[0, peer]
        both = packed[peer]
        rows, cols = word_taps(both[0:1], taps, word)
        for part, value in enumerate(predict(whole, rows, cols, word)):
            ready[peer, 0, part] = value
        ready[peer, 1] = late[peer]

    def home(peer):
        return pltpu.make_async_remote_copy(
            src_ref=ready.at[pl.ds(peer, 1)],
            dst_ref=back.at[pl.ds(me, 1)],
            send_sem=b_sems.at[0],
            recv_sem=b_sems.at[1],
            device_id={"tile": peer},
            device_id_type=MESH,
        )

    def make_group(group):
        for k in range(WIDTH):
            make((me + 1 + group * WIDTH + k) % TILES)

    def send_group(group, width):
        for k in range(width):
            home((me + 1 + group * WIDTH + k) % TILES).start()

    def turn(group, carry):
        make_group(group)
        send_group(group, WIDTH)
        return carry

    make_group(0)
    pl.semaphore_wait(barrier, TILES - 1 + CHAN - 1)
    send_group(0, WIDTH)
    for k in range(1, CHAN):
        across(k).start()
    last = TILES // WIDTH - 1
    lax.fori_loop(1, last, turn, 0)
    make_group(last)
    send_group(last, WIDTH - 1)
    back[me] = ready[me]
    total = summed[:, rows_of(chan), :]
    for k in range(1, CHAN):
        across(k).wait()
        total = total + parts[k - 1]
    combined[...] = total
    most = ready.at[pl.ds(0, TILES - 1)]
    for k in range(2):
        pltpu.make_async_copy(most, most, b_sems.at[k]).wait()
    for first in range(0, 16, 4):
        results = []
        for b in range(first, first + 4):
            word = info[b]
            keep = ((word >> 9) & 1).astype(jnp.float32)
            flip = (1 - 2 * ((word >> 8) & 1)).astype(jnp.float32)
            for part in range(2):
                value = back[(word >> 1) & 63, word & 1, part].astype(jnp.float32)
                value = jnp.where(keep > 0.5, value * flip if part else value, jnp.float32(0.0))
                results.append((vis[b, part].astype(jnp.float32) - value).astype(jnp.bfloat16))
        for k, result in enumerate(results):
            residual[first + k // 2, k % 2] = result


def send_back(info, heads, late, packed, table, whole, vis, summed):
    slots = (TILES, 2, 2, 2, BLOCK)
    return pl.pallas_call(
        back_kernel,
        out_shape=(
            jax.ShapeDtypeStruct(vis.shape, vis.dtype),
            jax.ShapeDtypeStruct((2, TS // CHAN, TS), jnp.float32),
        ),
        in_specs=[SMEM, SMEM, VMEM, VMEM, VMEM, VMEM, VMEM, VMEM],
        out_specs=(VMEM, VMEM),
        scratch_shapes=[
            pltpu.VMEM(slots, jnp.bfloat16),
            pltpu.VMEM(slots, jnp.bfloat16),
            pltpu.VMEM((CHAN - 1, 2, TS // CHAN, TS), jnp.float32),
            pltpu.SemaphoreType.DMA((2,)),
            pltpu.SemaphoreType.DMA((CHAN - 1,)),
            pltpu.SemaphoreType.DMA((CHAN - 1,)),
        ],
        compiler_params=pltpu.CompilerParams(
            collective_id=2, has_side_effects=True, vmem_limit_bytes=LIMIT
        ),
        name="send_back",
    )(info, heads, late, packed, table, whole, vis, summed)


def per_device(visibility, imaging_weight, position, anchor, destination, block_count, kernel):
    scaled, packed, info, table = sort_blocks(
        destination, block_count, anchor.T, visibility, imaging_weight, position, kernel.T
    )
    scaled, packed = route(scaled, packed)
    grid, heads, late = grid_blocks(scaled, packed, table)
    whole, summed = join_grids(grid)
    whole = whole.reshape(2, 4, TS // 16, 16, TS)
    predicted, framed = degrid_late(late, heads, packed, table, whole, summed)
    residual, combined = send_back(
        info, heads, predicted, packed, table, whole, visibility, framed
    )
    return combined, residual


def solution(mesh):
    placed = (
        P("tile", None, "chan", None),
        P("tile", "chan", None),
        P("tile", None, None),
        P("tile", None),
        P("tile"),
        P("tile"),
        P(),
    )
    return jax.shard_map(
        per_device,
        mesh=mesh,
        in_specs=placed,
        out_specs=(P(None, ("tile", "chan"), None), P("tile", None, "chan", None)),
        check_vma=False,
    )
```

```python
import functools

import jax
import jax.numpy as jnp
from jax import lax
from jax.experimental import pallas as pl
from jax.experimental.pallas import tpu as pltpu
from jax.sharding import PartitionSpec as P

BLOCK = 512
TAPS = 16
OS = 32
SUB = 128
TS = 256
TILES = 64
CHAN = 4
SLOTS = 128
ROWS = 144
GROUPS = 4
WIDTH = 8
LIMIT = 16 * 1024 * 1024

VMEM = pl.BlockSpec(memory_space=pltpu.VMEM)
SMEM = pl.BlockSpec(memory_space=pltpu.SMEM)
HBM = pl.BlockSpec(memory_space=pltpu.HBM)
MESH = pl.DeviceIdType.MESH


def sort_kernel(
    far_dest,
    count,
    far_anchor,
    far_vis,
    far_weight,
    far_pos,
    far_kernel,
    scaled,
    packed,
    info,
    table,
    used,
    dest,
    anchor,
    vis,
    weight,
    pos,
    kernel,
    sems,
):
    fetches = [
        pltpu.make_async_copy(source, target, sems.at[k])
        for k, (source, target) in enumerate(
            (
                (far_dest, dest),
                (far_anchor, anchor),
                (far_vis, vis),
                (far_weight, weight),
                (far_pos, pos),
                (far_kernel, kernel),
            )
        )
    ]
    for fetch in fetches:
        fetch.start()
    me = lax.axis_index("tile")
    turn = me + (me >> 2) + (me >> 4)
    scaled[...] = jnp.zeros(scaled.shape, scaled.dtype)
    packed[...] = jnp.zeros(packed.shape, packed.dtype)
    for quad in range(TILES // 4):
        used[quad] = 0

    def ones_where(mask):
        return jnp.where(mask, jnp.float32(1.0), jnp.float32(0.0)).astype(jnp.bfloat16)

    def iota(shape, axis):
        return lax.broadcasted_iota(jnp.int32, shape, axis)

    fetches[5].wait()
    values = kernel[...].astype(jnp.bfloat16)
    swap = ones_where(iota((TAPS, TAPS), 0) + iota((TAPS, TAPS), 1) == TAPS - 1)
    turned = jnp.dot(swap, values, preferred_element_type=jnp.float32).astype(jnp.bfloat16)
    spread = iota((OS, 128), 1) - iota((OS, 128), 0)
    table[...] = jnp.dot(
        values, ones_where(spread == 0), preferred_element_type=jnp.float32
    ) + jnp.dot(turned, ones_where(spread == OS), preferred_element_type=jnp.float32)
    for fetch in fetches[:5]:
        fetch.wait()
    for b in range(16):
        alive = (b < count[0]).astype(jnp.int32)
        tile = dest[b]
        quad = (tile & 31) >> 1
        rank = used[quad]
        used[quad] = rank + alive
        member = (rank + turn) & 3
        device = (quad << 1) | (member & 1) | ((member >> 1) << 5)
        which = rank >> 2
        mirror = tile >> 5
        flip = 1 - 2 * mirror
        top = mirror * (TS - SUB) + flip * anchor[0, b]
        left = mirror * (TS - SUB) + flip * anchor[1, b]
        base = jnp.minimum(top >> 4, 7)
        info[b] = (device * 2 + which) | (mirror << 8) | (alive << 9)
        meta = (alive << 26) | (base << 27) | (mirror << 30) | ((tile & 1) << 31)

        @pl.when(alive == 1)
        def _():
            place = pos[b]
            cell = mirror * (SUB - TAPS) + flip * (place >> 5)
            offset = place & (OS - 1)
            row = (cell[0:1] + (top - base * 16)) * OS + offset[0:1]
            column = (cell[1:2] + left) * OS + offset[1:2]
            packed[device, pl.ds(which, 1), :] = row | (column << 13) | meta
            factor = weight[b].astype(jnp.float32)
            sign = flip.astype(jnp.float32)
            slot = device * 2 + which
            scaled[slot, 0] = (vis[b, 0].astype(jnp.float32) * factor).astype(jnp.bfloat16)
            scaled[slot, 1] = (vis[b, 1].astype(jnp.float32) * (factor * sign)).astype(jnp.bfloat16)


def in_hbm(array):
    return pltpu.with_memory_space_constraint(array, pltpu.HBM)


def sort_blocks(dest, count, anchor, vis, weight, pos, kernel):
    return pl.pallas_call(
        sort_kernel,
        out_shape=(
            jax.ShapeDtypeStruct((SLOTS, 2, 2, BLOCK), jnp.bfloat16),
            jax.ShapeDtypeStruct((TILES, 2, BLOCK), jnp.int32),
            jax.ShapeDtypeStruct((16,), jnp.int32),
            jax.ShapeDtypeStruct((TAPS, 128), jnp.float32),
        ),
        in_specs=[HBM, SMEM, HBM, HBM, HBM, HBM, HBM],
        out_specs=(VMEM, VMEM, SMEM, VMEM),
        scratch_shapes=[
            pltpu.SMEM((TILES // 4,), jnp.int32),
            pltpu.SMEM(dest.shape, dest.dtype),
            pltpu.SMEM(anchor.shape, anchor.dtype),
            pltpu.VMEM(vis.shape, vis.dtype),
            pltpu.VMEM(weight.shape, weight.dtype),
            pltpu.VMEM(pos.shape, pos.dtype),
            pltpu.VMEM(kernel.shape, kernel.dtype),
            pltpu.SemaphoreType.DMA((6,)),
        ],
        compiler_params=pltpu.CompilerParams(vmem_limit_bytes=LIMIT),
        name="sort_blocks",
    )(in_hbm(dest), count, *map(in_hbm, (anchor, vis, weight, pos, kernel)))


def greet_tiles(me):
    barrier = pltpu.get_barrier_semaphore()

    def greet(step, carry):
        pl.semaphore_signal(
            barrier, inc=1, device_id={"tile": (me + step) % TILES}, device_id_type=MESH
        )
        return carry

    lax.fori_loop(1, TILES, greet, 0)
    return barrier


def route_kernel(scaled, packed, table, got_scaled, got_packed, row_taps, col_taps, sems, here):
    me = lax.axis_index("tile")
    pl.semaphore_wait(greet_tiles(me), TILES - 1)

    def values_copy(peer):
        return pltpu.make_async_remote_copy(
            src_ref=scaled.at[pl.ds(peer * 2, 2)],
            dst_ref=got_scaled.at[pl.ds(me * 2, 2)],
            send_sem=sems.at[0],
            recv_sem=sems.at[1],
            device_id={"tile": peer},
            device_id_type=MESH,
        )

    def places_copy(peer):
        return pltpu.make_async_remote_copy(
            src_ref=packed.at[pl.ds(peer, 1)],
            dst_ref=got_packed.at[pl.ds(me, 1)],
            send_sem=sems.at[2],
            recv_sem=sems.at[3],
            device_id={"tile": peer},
            device_id_type=MESH,
        )

    def send_places(step, carry):
        places_copy((me + step) % TILES).start()
        return carry

    def send_values(step, carry):
        values_copy((me + step) % TILES).start()
        return carry

    lax.fori_loop(1, TILES, send_places, 0)
    lax.fori_loop(1, TILES, send_values, 0)
    own_scaled = pltpu.make_async_copy(
        scaled.at[pl.ds(me * 2, 2)], got_scaled.at[pl.ds(me * 2, 2)], here.at[0]
    )
    own_packed = pltpu.make_async_copy(
        packed.at[pl.ds(me, 1)], got_packed.at[pl.ds(me, 1)], here.at[1]
    )
    own_scaled.start()
    own_packed.start()
    own_scaled.wait()
    own_packed.wait()

    most_scaled = scaled.at[pl.ds(0, SLOTS - 2)]
    most_packed = packed.at[pl.ds(0, TILES - 1)]
    pltpu.make_async_copy(most_packed, most_packed, sems.at[3]).wait()
    taps = table[...]

    def build(group, carry):
        for k in range(4):
            device = group * 4 + k
            places = got_packed[device]
            rows, cols = word_taps(places[0:1], taps, (places[0:1, 0:128] >> 30) & 1)
            row_taps[device] = jnp.concatenate(
                [jnp.concatenate(tiles, axis=0) for tiles in rows], axis=1
            )
            col_taps[device] = cols
        return carry

    lax.fori_loop(0, TILES // 4, build, 0)
    for k, most in enumerate((most_scaled, most_scaled, most_packed)):
        pltpu.make_async_copy(most, most, sems.at[k]).wait()


def route(scaled, packed, table):
    return pl.pallas_call(
        route_kernel,
        out_shape=(
            jax.ShapeDtypeStruct(scaled.shape, scaled.dtype),
            jax.ShapeDtypeStruct(packed.shape, packed.dtype),
            jax.ShapeDtypeStruct((TILES, ROWS, BLOCK), jnp.bfloat16),
            jax.ShapeDtypeStruct((TILES, TS, BLOCK), jnp.bfloat16),
        ),
        in_specs=[VMEM, VMEM, VMEM],
        out_specs=(VMEM, VMEM, VMEM, VMEM),
        scratch_shapes=[pltpu.SemaphoreType.DMA((4,)), pltpu.SemaphoreType.DMA((2,))],
        compiler_params=pltpu.CompilerParams(
            collective_id=0, has_side_effects=True, vmem_limit_bytes=LIMIT
        ),
        name="route",
    )(scaled, packed, table)


def live_turns(count, one):
    def many(start, width):
        def step(turn, carry):
            for k in range(width):
                at = start + turn * width + k
                one(jnp.where(at < count, at, 0), at < count)
            return carry

        return step

    eights = count >> 3
    lax.fori_loop(0, eights, many(0, 8), 0)
    lax.fori_loop(0, (count - eights * 8 + 1) >> 1, many(eights * 8, 2), 0)


def tap_tiles(table, cell, column, pieces):
    cell = jnp.broadcast_to(cell, (8, 128))
    column = jnp.broadcast_to(column, (8, 128))
    low = jnp.take_along_axis(table[:8], column, axis=1, mode="promise_in_bounds")
    high = jnp.take_along_axis(table[8:], column, axis=1, mode="promise_in_bounds")
    sub = lax.broadcasted_iota(jnp.int32, (8, 128), 0)
    part = cell & 7
    turn = (sub - part) & 7
    low = jnp.take_along_axis(low, turn, axis=0, mode="promise_in_bounds")
    high = jnp.take_along_axis(high, turn, axis=0, mode="promise_in_bounds")
    after = sub >= part
    zero = jnp.zeros((8, 128), jnp.float32)
    first = jnp.where(after, low, zero)
    second = jnp.where(after, high, low)
    third = jnp.where(after, zero, high)
    late = (cell & 8) == 8

    def both(upper, lower):
        return jnp.concatenate([upper, lower], axis=0).astype(jnp.bfloat16)

    begin = both(jnp.where(late, zero, first), jnp.where(late, first, second))
    end = both(jnp.where(late, second, third), jnp.where(late, third, zero))
    whole = (cell >> 4).astype(jnp.float32)
    whole = both(whole, whole)
    blank = jnp.zeros((16, 128), jnp.bfloat16)
    at = [whole == jnp.bfloat16(m) for m in range(pieces)]
    tiles = []
    for m in range(pieces):
        value = jnp.where(at[m - 1], end, blank) if m else blank
        tiles.append(jnp.where(at[m], begin, value))
    return tiles


def slot_taps(packed, table, slot, word):
    both = packed[slot >> 1]
    mine = jnp.where((slot & 1) == 1, both[1:2], both[0:1])
    return word_taps(mine, table, (word >> 30) & 1)


def word_taps(mine, table, mirror):
    shift = OS * mirror
    if getattr(mirror, "shape", ()):
        shift = jnp.concatenate([shift] * GROUPS, axis=1)
    row_cell = (mine >> 5) & 255
    row_column = (mine & (OS - 1)) + shift
    col_cell = (mine >> 18) & 255
    col_column = ((mine >> 13) & (OS - 1)) + shift
    lanes = [slice(g * 128, (g + 1) * 128) for g in range(GROUPS)]
    rows = [tap_tiles(table, row_cell[:, k], row_column[:, k], ROWS // 16) for k in lanes]
    cols = [
        jnp.concatenate(tap_tiles(table, col_cell[:, k], col_column[:, k], TS // 16), axis=0)
        for k in lanes
    ]
    return rows, jnp.concatenate(cols, axis=1)


def grid_kernel(scaled, packed, table, row_taps, col_taps, grid, heads, late, line, live, sem):
    flags = jnp.concatenate([packed[:, 0, 0:128], packed[:, 1, 0:128]], axis=0)
    line[...] = jnp.broadcast_to(flags.T[0:1], (8, 128))
    fetch = pltpu.make_async_copy(line, heads, sem)
    fetch.start()
    grid[...] = jnp.zeros(grid.shape, grid.dtype)
    taps = table[...]
    fetch.wait()

    def look(device, counts):
        count, extra = counts
        live[count] = device
        late[extra] = device
        return count + ((heads[0, device] >> 26) & 1), extra + (
            (heads[0, TILES + device] >> 26) & 1
        )

    count, extra = lax.fori_loop(0, TILES, look, (jnp.int32(0), jnp.int32(0)), unroll=4)
    late[TILES] = extra

    def one(k, alive):
        device = live[k]
        rows = row_taps[device]
        rows = [
            [rows[m * 16 : m * 16 + 16, g * 128 : g * 128 + 128] for m in range(ROWS // 16)]
            for g in range(GROUPS)
        ]
        add(device * 2, heads[0, device], alive, rows, col_taps[device])

    def one_late(k, carry):
        device = late[k]
        slot, word = device * 2 + 1, heads[0, TILES + device]
        add(slot, word, jnp.bool_(True), *slot_taps(packed, taps, slot, word))
        return carry

    def add(slot, word, alive, rows, cols):
        keep = alive.astype(jnp.float32)
        planes = []
        for part in range(2):
            values = scaled[slot, part].astype(jnp.float32) * keep
            for channel in range(2):
                lanes = []
                for g in range(GROUPS):
                    value = values[channel : channel + 1, g * 128 : (g + 1) * 128]
                    value = jnp.broadcast_to(value, (16, 128)).astype(jnp.bfloat16)
                    lanes.append(jnp.concatenate([tile * value for tile in rows[g]], axis=0))
                planes.append(jnp.concatenate(lanes, axis=1))
        product = lax.dot_general(
            jnp.concatenate(planes, axis=0),
            cols,
            (((1,), (1,)), ((), ())),
            preferred_element_type=jnp.float32,
        )
        pair = (word >> 31) & 1
        start = pl.multiple_of(((word >> 27) & 7) * 16, 16)
        for plane in range(4):
            grid[pair, plane, pl.ds(start, ROWS), :] += product[plane * ROWS : (plane + 1) * ROWS]

    live_turns(count, one)
    lax.fori_loop(0, extra, one_late, 0)


def grid_blocks(scaled, packed, table, row_taps, col_taps):
    return pl.pallas_call(
        grid_kernel,
        out_shape=(
            jax.ShapeDtypeStruct((2, 4, TS, TS), jnp.float32),
            jax.ShapeDtypeStruct((8, 128), jnp.int32),
            jax.ShapeDtypeStruct((TILES + 8,), jnp.int32),
        ),
        in_specs=[VMEM, VMEM, VMEM, VMEM, VMEM],
        out_specs=(VMEM, SMEM, SMEM),
        scratch_shapes=[
            pltpu.VMEM((8, 128), jnp.int32),
            pltpu.SMEM((SLOTS + 8,), jnp.int32),
            pltpu.SemaphoreType.DMA,
        ],
        compiler_params=pltpu.CompilerParams(vmem_limit_bytes=LIMIT),
        name="grid_blocks",
    )(scaled, packed, table, row_taps, col_taps)


def join_kernel(grid, whole, summed, half, got_half, total, mine, got_mine, send, recv):
    me = lax.axis_index("tile")
    core = me & 1
    near = me ^ 1
    far = me ^ (TILES // 2)
    barrier = pltpu.get_barrier_semaphore()
    for peer in (near, far):
        pl.semaphore_signal(barrier, inc=1, device_id={"tile": peer}, device_id_type=MESH)

    def pass_on(source, target, sem, peer):
        return pltpu.make_async_remote_copy(
            src_ref=source,
            dst_ref=target,
            send_sem=send.at[sem],
            recv_sem=recv.at[sem],
            device_id={"tile": peer},
            device_id_type=MESH,
        )

    for k in range(4):
        half[k] = grid[1 - core, k].astype(jnp.bfloat16)
    pl.semaphore_wait(barrier, 2)
    first = [pass_on(half.at[k], got_half.at[k], k, near) for k in range(4)]
    second = [pass_on(mine.at[k], got_mine.at[k], 4 + k, far) for k in range(4)]
    third = [pass_on(whole.at[core, k], whole.at[core, k], 8 + k, near) for k in range(4)]
    for k in range(4):
        first[k].start()
    for k in range(4):
        first[k].wait_recv()
        value = grid[core, k] + got_half[k].astype(jnp.float32)
        total[k] = value
        mine[k] = value.astype(jnp.bfloat16)
        second[k].start()
    for k in range(4):
        second[k].wait_recv()
        value = total[k] + got_mine[k].astype(jnp.float32)
        whole[core, k] = value.astype(jnp.bfloat16)
        third[k].start()
        if k % 2 == 0:
            summed[k // 2] = value
        else:
            summed[k // 2] += value
    for k in range(4):
        other = pltpu.make_async_copy(whole.at[1 - core, k], whole.at[1 - core, k], recv.at[8 + k])
        other.wait()
        first[k].wait_send()
        second[k].wait_send()
        third[k].wait_send()


def join_grids(grid):
    return pl.pallas_call(
        join_kernel,
        out_shape=(
            jax.ShapeDtypeStruct((2, 4, TS, TS), jnp.bfloat16),
            jax.ShapeDtypeStruct((2, TS, TS), jnp.float32),
        ),
        in_specs=[VMEM],
        out_specs=(VMEM, VMEM),
        scratch_shapes=[
            pltpu.VMEM((4, TS, TS), jnp.bfloat16),
            pltpu.VMEM((4, TS, TS), jnp.bfloat16),
            pltpu.VMEM((4, TS, TS), jnp.float32),
            pltpu.VMEM((4, TS, TS), jnp.bfloat16),
            pltpu.VMEM((4, TS, TS), jnp.bfloat16),
            pltpu.SemaphoreType.DMA((12,)),
            pltpu.SemaphoreType.DMA((12,)),
        ],
        compiler_params=pltpu.CompilerParams(
            collective_id=1, has_side_effects=True, vmem_limit_bytes=LIMIT
        ),
        name="join_grids",
    )(grid)


def turn_over(value):
    sub = lax.broadcasted_iota(jnp.int32, (8, 128), 0)
    lane = lax.broadcasted_iota(jnp.int32, (8, 128), 1)

    def reverse(tile):
        tile = jnp.take_along_axis(tile, 127 - lane, axis=1, mode="promise_in_bounds")
        return jnp.take_along_axis(tile, 7 - sub, axis=0, mode="promise_in_bounds")

    rows = []
    for m in reversed(range(TS // 8)):
        tiles = [reverse(value[m * 8 : m * 8 + 8, k * 128 : k * 128 + 128]) for k in (1, 0)]
        rows.append(jnp.concatenate(tiles, axis=1))
    return jnp.concatenate(rows, axis=0)


def predict(whole, rows, cols, word):
    pair = (word >> 31) & 1
    base = (word >> 27) & 7
    scale = jnp.float32(1.0 / (TAPS * TAPS))
    parts = []
    for part in range(2):
        results = []
        for channel in range(2):
            plane = part * 2 + channel
            window = jnp.concatenate(
                [whole[pair, plane, base + k] for k in range(ROWS // 16)], axis=0
            )
            across = jnp.dot(window, cols, preferred_element_type=jnp.float32)
            sums = [
                jnp.sum(rows[g] * across[:, g * 128 : (g + 1) * 128], axis=0, keepdims=True)
                for g in range(GROUPS)
            ]
            results.append(jnp.concatenate(sums, axis=1))
        parts.append((jnp.concatenate(results, axis=0) * scale).astype(jnp.bfloat16))
    return parts


def late_kernel(late, heads, packed, table, whole, summed, predicted, framed):
    upper = lax.axis_index("tile") // (TILES // 2)
    taps = table[...]

    @pl.when(upper == 1)
    def _():
        framed[0] = turn_over(summed[0])
        framed[1] = -turn_over(summed[1])

    @pl.when(upper == 0)
    def _():
        framed[...] = summed[...]

    predicted[...] = jnp.zeros(predicted.shape, predicted.dtype)

    def one(k, carry):
        device = late[k]
        word = heads[0, TILES + device]
        rows, cols = slot_taps(packed, taps, device * 2 + 1, word)
        rows = [jnp.concatenate(tiles, axis=0).astype(jnp.float32) for tiles in rows]
        for part, value in enumerate(predict(whole, rows, cols, word)):
            predicted[device, part] = value
        return carry

    lax.fori_loop(0, late[TILES], one, 0)


def degrid_late(late, heads, packed, table, whole, summed):
    return pl.pallas_call(
        late_kernel,
        out_shape=(
            jax.ShapeDtypeStruct((TILES, 2, 2, BLOCK), jnp.bfloat16),
            jax.ShapeDtypeStruct((2, TS, TS), jnp.float32),
        ),
        in_specs=[SMEM, SMEM, VMEM, VMEM, VMEM, VMEM],
        out_specs=(VMEM, VMEM),
        compiler_params=pltpu.CompilerParams(vmem_limit_bytes=LIMIT),
        name="degrid_late",
    )(late, heads, packed, table, whole, summed)


def back_kernel(
    info,
    heads,
    late,
    row_taps,
    col_taps,
    whole,
    vis,
    summed,
    residual,
    combined,
    ready,
    back,
    parts,
    b_sems,
    c_out,
    c_in,
):
    me = lax.axis_index("tile")
    chan = lax.axis_index("chan")
    barrier = greet_tiles(me)
    for k in range(1, CHAN):
        pl.semaphore_signal(
            barrier, inc=1, device_id={"chan": (chan + k) % CHAN}, device_id_type=MESH
        )

    def rows_of(group):
        return pl.ds(pl.multiple_of(group * (TS // CHAN), TS // CHAN), TS // CHAN)

    def across(k):
        group = (chan + k) % CHAN
        return pltpu.make_async_remote_copy(
            src_ref=summed.at[:, rows_of(group), :],
            dst_ref=parts.at[k - 1],
            send_sem=c_out.at[k - 1],
            recv_sem=c_in.at[k - 1],
            device_id={"chan": group},
            device_id_type=MESH,
        )

    def make(peer):
        rows = row_taps[peer].astype(jnp.float32)
        rows = [rows[:, g * 128 : g * 128 + 128] for g in range(GROUPS)]
        for part, value in enumerate(predict(whole, rows, col_taps[peer], heads[0, peer])):
            ready[peer, 0, part] = value
        ready[peer, 1] = late[peer]

    def home(peer):
        return pltpu.make_async_remote_copy(
            src_ref=ready.at[pl.ds(peer, 1)],
            dst_ref=back.at[pl.ds(me, 1)],
            send_sem=b_sems.at[0],
            recv_sem=b_sems.at[1],
            device_id={"tile": peer},
            device_id_type=MESH,
        )

    def make_group(group):
        for k in range(WIDTH):
            make((me + 1 + group * WIDTH + k) % TILES)

    def send_group(group, width):
        for k in range(width):
            home((me + 1 + group * WIDTH + k) % TILES).start()

    def turn(group, carry):
        make_group(group)
        send_group(group, WIDTH)
        return carry

    make_group(0)
    pl.semaphore_wait(barrier, TILES - 1 + CHAN - 1)
    send_group(0, WIDTH)
    for k in range(1, CHAN):
        across(k).start()
    last = TILES // WIDTH - 1
    lax.fori_loop(1, last, turn, 0)
    make_group(last)
    send_group(last, WIDTH - 1)
    back[me] = ready[me]
    total = summed[:, rows_of(chan), :]
    for k in range(1, CHAN):
        across(k).wait()
        total = total + parts[k - 1]
    combined[...] = total
    most = ready.at[pl.ds(0, TILES - 1)]
    for k in range(2):
        pltpu.make_async_copy(most, most, b_sems.at[k]).wait()
    for first in range(0, 16, 4):
        results = []
        for b in range(first, first + 4):
            word = info[b]
            keep = ((word >> 9) & 1).astype(jnp.float32)
            flip = (1 - 2 * ((word >> 8) & 1)).astype(jnp.float32)
            for part in range(2):
                value = back[(word >> 1) & 63, word & 1, part].astype(jnp.float32)
                value = jnp.where(keep > 0.5, value * flip if part else value, jnp.float32(0.0))
                results.append((vis[b, part].astype(jnp.float32) - value).astype(jnp.bfloat16))
        for k, result in enumerate(results):
            residual[first + k // 2, k % 2] = result


def send_back(info, heads, late, row_taps, col_taps, whole, vis, summed):
    slots = (TILES, 2, 2, 2, BLOCK)
    return pl.pallas_call(
        back_kernel,
        out_shape=(
            jax.ShapeDtypeStruct(vis.shape, vis.dtype),
            jax.ShapeDtypeStruct((2, TS // CHAN, TS), jnp.float32),
        ),
        in_specs=[SMEM, SMEM, VMEM, VMEM, VMEM, VMEM, VMEM, VMEM],
        out_specs=(VMEM, VMEM),
        scratch_shapes=[
            pltpu.VMEM(slots, jnp.bfloat16),
            pltpu.VMEM(slots, jnp.bfloat16),
            pltpu.VMEM((CHAN - 1, 2, TS // CHAN, TS), jnp.float32),
            pltpu.SemaphoreType.DMA((2,)),
            pltpu.SemaphoreType.DMA((CHAN - 1,)),
            pltpu.SemaphoreType.DMA((CHAN - 1,)),
        ],
        compiler_params=pltpu.CompilerParams(
            collective_id=2, has_side_effects=True, vmem_limit_bytes=LIMIT
        ),
        name="send_back",
    )(info, heads, late, row_taps, col_taps, whole, vis, summed)


def per_device(visibility, imaging_weight, position, anchor, destination, block_count, kernel):
    scaled, packed, info, table = sort_blocks(
        destination, block_count, anchor.T, visibility, imaging_weight, position, kernel.T
    )
    scaled, packed, row_taps, col_taps = route(scaled, packed, table)
    grid, heads, late = grid_blocks(scaled, packed, table, row_taps, col_taps)
    whole, summed = join_grids(grid)
    whole = whole.reshape(2, 4, TS // 16, 16, TS)
    predicted, framed = degrid_late(late, heads, packed, table, whole, summed)
    residual, combined = send_back(
        info, heads, predicted, row_taps, col_taps, whole, visibility, framed
    )
    return combined, residual


def solution(mesh):
    placed = (
        P("tile", None, "chan", None),
        P("tile", "chan", None),
        P("tile", None, None),
        P("tile", None),
        P("tile"),
        P("tile"),
        P(),
    )
    return jax.shard_map(
        per_device,
        mesh=mesh,
        in_specs=placed,
        out_specs=(P(None, ("tile", "chan"), None), P("tile", None, "chan", None)),
        check_vma=False,
    )
```
